32 devices in a mesh: runs: 2 (over y), patch: 4 (over x, core), col: 4 (over z).
Axes of the slice: x: 2, y: 2, z: 4, core: 2. Of those that a mesh axis runs over, the one named last changes fastest.
Arguments:
- velocity: float32 [512, 3, 8192], P('runs', None, 'patch'), parts along dimension 0, may hold values from -6 to 6
- state: float32 [512, 8192], P(('runs', 'col'), 'patch'), parts along dimension 0, may hold values from 0.5 to 2
- friction: float32 [6, 8192], P('runs', 'patch'), parts along dimension 0, may hold values from 0.5 to 2
- near_src: int32 [64, 8], P('patch', 'col'), may hold values from 0 to 63, as said below
- near_block: bfloat16 [64, 8, 384, 384], P('patch', 'col'), may hold values from -0.109375 to 0.109375
- far_dest: int32 [4, 64, 4], P('col', 'patch'), may hold values from 0 to 127, as said below
- far_rank: int32 [4, 64, 4], P('col', 'patch'), may hold values from 1 to 32
- far_basis_v: bfloat16 [4, 64, 4, 32, 384], P('col', 'patch'), may hold values from -0.3125 to 0.3125
- far_target: int32 [4, 4, 4, 32], P('col', 'patch'), may hold values from -1 to 15, as said below
- far_basis_u: bfloat16 [4, 4, 4, 32, 32, 384], P('col', 'patch'), may hold values from -0.25 to 0.25
Outputs:
- velocity_rate: float32 [512, 3, 8192], P(('runs', 'col'), None, 'patch'), parts along dimension 0
The draws below stay inside these ranges and needn't reach their ends.
There are 2 independent parts, one for each index of `runs`. The reference program is written for one: setup_inputs(seed, part) draws one part's arguments, and reference() takes and returns one part's arrays. A program takes and returns all parts, laid end to end along the dimension named above; an argument that names none is the same for every part. Nothing has to cross between parts.
Inputs may be any that keep to these rules, and one draw needn't show every extreme that they name: `near_src`: entry 0 of each row is the target cluster itself; every entry lies within 16 clusters of its target cluster; the last entry lies exactly 16 clusters away. `far_dest`: for one c and the source clusters of one index of patch the slot numbers are distinct, and one target row p gets all 32 numbers p * 32 to p * 32 + 31. far_target[c, p, q, s] is the local index within target row p of the target cluster of the far block of list c from source row q with slot number p * 32 + s, and -1 where no block has that slot.
All inputs are finite; a program needn't handle non-finite values.
Results may differ from the reference program's by a relative error of at most 0.0026.
Values may be sent and summed in bfloat16 or wider, within the bound.
A program may use at most 192 MiB of HBM per device.

```python
import math
import jax
import jax.numpy as jnp
from jax import lax

CS = 128
TC = 16
MEM = 256
RK = 32
NBD = 2
NFD = 4
REACH = 16
NCL = 64
NE = 8192
NB = 8
CAP = 32
N_PATCH = 4
N_COL = 4


def far_layout(key):
    slot_total = N_PATCH * CAP
    block_count = TC * NFD
    device_keys = jax.random.split(key, N_COL * N_PATCH)

    def one_device(dev_key):
        key_row, key_score, key_perm, key_target = jax.random.split(dev_key, 4)
        full_row = jax.random.randint(key_row, (), 0, N_PATCH)
        slot_ids = jnp.arange(slot_total, dtype=jnp.int32)
        scores = jax.random.randint(key_score, (slot_total,), 0, 65536) * slot_total + slot_ids
        scores = scores + jnp.where(slot_ids // CAP == full_row, 1 << 28, 0)
        ranked = jnp.argsort(-scores, stable=True)
        chosen = ranked[:block_count].astype(jnp.int32)
        chosen = chosen[jax.random.permutation(key_perm, block_count)]
        filled = jnp.zeros((slot_total,), jnp.int32).at[chosen].set(1)
        targets = jax.random.randint(key_target, (slot_total,), 0, TC)
        local_target = jnp.where(filled > 0, targets, -1)
        return (chosen.reshape(TC, NFD), local_target.reshape(N_PATCH, CAP))
    dest_slots, local_target = jax.vmap(one_device)(device_keys)
    dest_slots = dest_slots.reshape(N_COL, N_PATCH * TC, NFD).astype(jnp.int32)
    local_target = local_target.reshape(N_COL, N_PATCH, N_PATCH, CAP)
    local_target = jnp.transpose(local_target, (0, 2, 1, 3)).astype(jnp.int32)
    return (dest_slots, local_target)


def draw_far_dest(key, part):
    return far_layout(key)[0]


def draw_far_target(key, part):
    return far_layout(key)[1]


def draw_near_src(key, part):
    key = jax.random.fold_in(key, 7)
    key_offset, key_flip = jax.random.split(key)
    clusters = TC * N_PATCH
    slot_count = NBD * N_COL
    centre = jnp.arange(clusters, dtype=jnp.int32)[:, None]
    offsets = jax.random.randint(key_offset, (clusters, slot_count), -REACH, REACH + 1)
    picked = jnp.clip(centre + offsets, 0, clusters - 1)
    flip_sign = 2 * jax.random.randint(key_flip, (clusters, 1), 0, 2) - 1
    far_end = centre + flip_sign * REACH
    far_end = jnp.where((far_end < 0) | (far_end > clusters - 1), centre - flip_sign * REACH, far_end)
    picked = picked.at[:, 0].set(centre[:, 0])
    picked = picked.at[:, slot_count - 1].set(far_end[:, 0])
    return picked.astype(jnp.int32)


def plant(drawn, key, smallest, largest):
    longest = drawn.shape.index(max(drawn.shape))
    spots = []
    for shift in (0, 1):
        where = [jax.random.randint(jax.random.fold_in(key, axis), (), 0, length) for axis, length in enumerate(drawn.shape)]
        where[longest] = (where[longest] + shift) % drawn.shape[longest]
        spots.append(tuple(where))
    return drawn.at[spots[0]].set(smallest).at[spots[1]].set(largest)


def steps_of(stream_key, extent, shards, least, high):
    factor_of = 1.0
    for axis_at, parts in shards:
        heights = jax.random.uniform(jax.random.fold_in(jax.random.fold_in(stream_key, 6), axis_at), (parts,), jnp.float32, least / len(shards), high / len(shards))
        factor_of = factor_of * jnp.repeat(jnp.exp(heights), extent[axis_at] // parts).reshape((-1,) + (1,) * (len(extent) - 1 - axis_at))
    return factor_of


def scatter_about(rng, shape, deviation, most, cuts=(), kind=jnp.bfloat16):
    entries = deviation * jax.random.normal(rng, shape, jnp.float32)
    if cuts:
        entries = entries * steps_of(rng, shape, cuts, -0.22, 0.18)
    return jnp.clip(entries, -most, most).astype(kind)


def setup_inputs(seed: int = 0, part: int = 0) -> dict:
    key_list = jax.random.split(jax.random.key(seed), 11)
    part_keys = jax.random.split(jax.random.fold_in(key_list[10], part), 11)
    return {
        "velocity": scatter_about(part_keys[0], (MEM, 3, NE), 1.0, 6.0, ((2, 4),), jnp.float32),
        "state": jnp.clip(jnp.exp(math.log(2.0) - 1.3862944 * jax.random.uniform(part_keys[1], (MEM, NE), jnp.float32) ** steps_of(part_keys[1], (MEM, NE), ((0, 4), (1, 4)), -0.2, 0.2)), 0.5, 2.0),
        "friction": jnp.clip(jnp.exp(math.log(2.0) - 1.3862944 * jax.random.uniform(part_keys[2], (3, NE), jnp.float32) ** steps_of(part_keys[2], (3, NE), ((1, 4),), -0.2, 0.2)), 0.5, 2.0),
        "near_src": draw_near_src(jax.random.fold_in(key_list[10], 71), part),
        "near_block": scatter_about(key_list[4], (NCL, NB, 3 * CS, 3 * CS), (3 * CS * NBD * N_COL) ** -0.5, 0.109375, ((0, 4), (1, 4))),
        "far_dest": draw_far_dest(jax.random.fold_in(key_list[10], 71), part),
        "far_rank": plant(jax.random.randint(key_list[6], (N_COL, NCL, NFD), 1, RK + 1), jax.random.fold_in(key_list[6], 1), 1, RK).astype(jnp.int32),
        "far_basis_v": scatter_about(key_list[7], (N_COL, NCL, NFD, RK, 3 * CS), (3 * CS) ** -0.5, 0.3125, ((0, 4), (1, 4))),
        "far_target": draw_far_target(jax.random.fold_in(key_list[10], 71), part),
        "far_basis_u": scatter_about(key_list[9], (N_COL, N_PATCH, N_PATCH, CAP, RK, 3 * CS), (RK * NFD * N_COL) ** -0.5, 0.25, ((0, 4), (1, 4))),
    }


damping = 0.5
speed_floor = 0.25

def reference(velocity, state, friction, near_src, near_block, far_dest, far_rank, far_basis_v, far_target, far_basis_u):
    clusters = NCL
    members = MEM
    rounded = velocity.astype(jnp.bfloat16)
    cluster_view = rounded.astype(jnp.float32).reshape(members, 3, clusters, CS)

    def near_slot(carry, slot_index):
        sources = near_src[:, slot_index]
        gathered = cluster_view[:, :, sources, :]
        blocks = lax.dynamic_index_in_dim(near_block, slot_index, 1, keepdims=False)
        blocks = blocks.astype(jnp.float32).reshape(clusters, 3, CS, 3, CS)
        return (carry + jnp.einsum('mcte,tadce->matd', gathered, blocks), None)
    near_stress, _ = lax.scan(near_slot, jnp.zeros((members, 3, clusters, CS), jnp.float32), jnp.arange(NB, dtype=jnp.int32))
    source_rows = (jnp.arange(clusters, dtype=jnp.int32) // TC)[:, None]
    rank_index = jnp.arange(RK, dtype=jnp.int32)

    def far_list(carry, column):
        basis = far_basis_v[column].astype(jnp.float32).reshape(clusters, NFD, RK, 3, CS)
        coeffs = jnp.einsum('gjkce,mcge->gjkm', basis, cluster_view)
        live_rank = (rank_index[None, None, :] < far_rank[column][:, :, None]).astype(jnp.float32)
        coeffs = lax.optimization_barrier((coeffs * live_rank[..., None]).astype(jnp.bfloat16)).astype(jnp.float32)
        dest_slots = far_dest[column]
        target_row = dest_slots // CAP
        position = dest_slots % CAP
        rows_source = jnp.broadcast_to(source_rows, dest_slots.shape)
        target_local = far_target[column][target_row, rows_source, position]
        targets = (target_row * TC + target_local).astype(jnp.int32)
        expand_basis = far_basis_u[column][target_row, rows_source, position]
        expand_basis = expand_basis.astype(jnp.float32).reshape(clusters, NFD, RK, 3, CS)
        terms = jnp.einsum('gjkm,gjkce->gjmce', coeffs, expand_basis).reshape(clusters * NFD, members, 3, CS)
        summed = jax.ops.segment_sum(terms, targets.reshape(-1), num_segments=clusters)
        return (carry + summed, None)
    far_stress, _ = lax.scan(far_list, jnp.zeros((clusters, members, 3, CS), jnp.float32), jnp.arange(N_COL, dtype=jnp.int32))
    far_stress = jnp.transpose(far_stress, (1, 2, 0, 3))
    stress = (near_stress + far_stress).reshape(members, 3, NE)
    direct_effect = friction[0][None, :]
    evolve_effect = friction[1][None, :]
    slip_length = friction[2][None, :]
    slip_speed = jnp.sqrt(lax.optimization_barrier(jnp.sum(velocity * velocity, axis=1)) + speed_floor)
    state_rate = 1.0 - slip_speed * state / slip_length
    pulled = evolve_effect * state_rate / (state * slip_speed)
    velocity_rate = (-stress - pulled[:, None, :] * velocity) / (direct_effect / slip_speed + damping)[:, None, :]
    return velocity_rate
```

```python
import functools
import jax
import jax.numpy as jnp
from jax import lax
from jax.experimental import pallas as pl
from jax.experimental.pallas import tpu as pltpu
from jax.sharding import PartitionSpec as P

CS = 128
CHUNKS = 2
GROUP = 8
MIB = 1 << 20

damping = 0.5
speed_floor = 0.25

NT = (((1,), (1,)), ((), ()))
TN = (((0,), (0,)), ((), ()))


def source_kernel(far_count, rank_width, dest_ref, rank_ref, vel_ref, basis_ref, own_ref, coef_ref):
    g = pl.program_id(0)
    members = own_ref.shape[1]
    for c in range(3):
        part = vel_ref[c].reshape(members, CS).astype(jnp.bfloat16)
        own_ref[0, :, c * CS : (c + 1) * CS] = part
    raw = lax.dot_general(basis_ref[0], own_ref[0], NT, preferred_element_type=jnp.float32)
    rows = lax.broadcasted_iota(jnp.int32, (rank_width, members), 0)
    for j in range(far_count):
        block = raw[j * rank_width : (j + 1) * rank_width]
        block = jnp.where(rows < rank_ref[g * far_count + j], block, 0.0)
        coef_ref[dest_ref[g * far_count + j]] = block.astype(jnp.bfloat16)


def source_step(chunk, velocity, basis_v, dest, rank):
    _, shares, _, sub, row_cells = velocity.shape
    members = shares * sub
    clusters = row_cells // CS
    far_count = dest.shape[0] // clusters
    rank_width = basis_v.shape[1] // far_count
    width = basis_v.shape[2]

    def call(slots):
        return pl.pallas_call(
            functools.partial(source_kernel, far_count, rank_width),
            grid_spec=pltpu.PrefetchScalarGridSpec(
                num_scalar_prefetch=2,
                grid=(clusters,),
                in_specs=[
                    pl.BlockSpec((3, shares, None, sub, CS), lambda g, *_: (0, 0, chunk, 0, g)),
                    pl.BlockSpec((1, far_count * rank_width, width), lambda g, *_: (g, 0, 0)),
                ],
                out_specs=[
                    pl.BlockSpec((1, members, width), lambda g, *_: (g, 0, 0)),
                    pl.BlockSpec((slots, rank_width, members), lambda g, *_: (0, 0, 0)),
                ],
            ),
            out_shape=[
                jax.ShapeDtypeStruct((clusters, members, width), jnp.bfloat16),
                jax.ShapeDtypeStruct((slots, rank_width, members), jnp.bfloat16),
            ],
            compiler_params=pltpu.CompilerParams(vmem_limit_bytes=24 * MIB),
            cost_estimate=pl.CostEstimate(
                flops=2 * clusters * far_count * rank_width * width * members,
                bytes_accessed=8 * MIB,
                transcendentals=0,
            ),
            name="source",
        )(dest, rank, velocity, basis_v)

    return call


def target_kernel(
    near_count, rank_width, src_ref, target_ref,
    left_ref, own_ref, right_ref, block_ref, coef_ref, basis_ref,
    out_ref, cells, acc, picked_c, picked_u, slot_list, slot_count, sems,
):
    t = pl.program_id(0)
    clusters = own_ref.shape[0]
    slots = coef_ref.shape[0]
    shares, _, sub, _ = out_ref.shape

    @pl.when(t == 0)
    def _():
        copies = [
            pltpu.make_async_copy(ref, cells.at[pl.ds(i * clusters, clusters)], sems.at[i])
            for i, ref in enumerate((left_ref, own_ref, right_ref))
        ]
        for copy in copies:
            copy.start()

        def clear(i, carry):
            slot_count[i] = 0
            return carry

        lax.fori_loop(0, clusters, clear, 0)

        def place(s, carry):
            goal = target_ref[s]

            @pl.when(goal >= 0)
            def _():
                at = slot_count[goal]
                slot_list[goal * slots + at] = s
                slot_count[goal] = at + 1

            return carry

        lax.fori_loop(0, slots, place, 0)
        for copy in copies:
            copy.wait()

    total = None
    for j in range(near_count):
        cell = cells[src_ref[t * near_count + j]]
        part = lax.dot_general(cell, block_ref[0, j], NT, preferred_element_type=jnp.float32)
        total = part if total is None else total + part
    acc[...] = total
    count = slot_count[t]

    def group(i, carry):
        for j in range(GROUP):
            at = i * GROUP + j
            live = at < count
            s = slot_list[t * slots + jnp.where(live, at, 0)]
            s = jnp.where(live, s, 0)
            piece = pl.ds(j * rank_width, rank_width)
            coef = coef_ref[s]
            picked_c[piece, :] = jnp.where(live, coef, jnp.zeros_like(coef))
            picked_u[piece, :] = basis_ref[s]
        acc[...] += lax.dot_general(
            picked_c[...], picked_u[...], TN, preferred_element_type=jnp.float32
        )
        return carry

    lax.fori_loop(0, (count + GROUP - 1) // GROUP, group, 0)
    for d in range(shares):
        for c in range(3):
            out_ref[d, c] = acc[d * sub : (d + 1) * sub, c * CS : (c + 1) * CS].astype(jnp.bfloat16)


def target_step(shares, src, target, left, own, right, blocks, coef, basis_u):
    clusters, members, width = own.shape
    near_count = blocks.shape[1]
    slots, rank_width, _ = coef.shape
    sub = members // shares
    whole = lambda t, *_: (0, 0, 0)
    return pl.pallas_call(
        functools.partial(target_kernel, near_count, rank_width),
        grid_spec=pltpu.PrefetchScalarGridSpec(
            num_scalar_prefetch=2,
            grid=(clusters,),
            in_specs=[
                pl.BlockSpec(memory_space=pl.ANY),
                pl.BlockSpec(memory_space=pl.ANY),
                pl.BlockSpec(memory_space=pl.ANY),
                pl.BlockSpec((1, near_count, width, width), lambda t, *_: (t, 0, 0, 0)),
                pl.BlockSpec((slots, rank_width, members), whole),
                pl.BlockSpec((slots, rank_width, width), whole),
            ],
            out_specs=pl.BlockSpec((shares, 3, sub, CS), lambda t, *_: (0, 0, 0, t)),
            scratch_shapes=[
                pltpu.VMEM((3 * clusters, members, width), jnp.bfloat16),
                pltpu.VMEM((members, width), jnp.float32),
                pltpu.VMEM((GROUP * rank_width, members), jnp.bfloat16),
                pltpu.VMEM((GROUP * rank_width, width), jnp.bfloat16),
                pltpu.SMEM((clusters * slots,), jnp.int32),
                pltpu.SMEM((clusters,), jnp.int32),
                pltpu.SemaphoreType.DMA((3,)),
            ],
        ),
        out_shape=jax.ShapeDtypeStruct((shares, 3, sub, clusters * CS), jnp.bfloat16),
        compiler_params=pltpu.CompilerParams(vmem_limit_bytes=36 * MIB),
        cost_estimate=pl.CostEstimate(
            flops=2 * clusters * members * width * (near_count * width + GROUP * rank_width),
            bytes_accessed=24 * MIB,
            transcendentals=0,
        ),
        name="target",
    )(src, target, left, own, right, blocks, coef, basis_u)


def law_kernel(chunks, col_ref, *refs):
    parts = refs[:chunks]
    vel_ref, state_ref, friction_ref, out_ref = refs[chunks:]
    sub = parts[0].shape[2]
    for h in range(chunks):
        rows = slice(h * sub, (h + 1) * sub)
        velocity = [vel_ref[c, rows, :] for c in range(3)]
        speed = jnp.sqrt(
            velocity[0] * velocity[0] + velocity[1] * velocity[1] + velocity[2] * velocity[2] + speed_floor
        )
        state = state_ref[rows, :]
        state_rate = 1.0 - speed * state / friction_ref[2:3, :]
        pulled = friction_ref[1:2, :] * state_rate / (state * speed)
        below = friction_ref[0:1, :] / speed + damping
        for c in range(3):
            stress = jnp.sum(parts[h][:, c].astype(jnp.float32), axis=0)
            out_ref[c, rows, :] = (-stress - pulled * velocity[c]) / below


def law_step(col, parts, velocity, state, friction):
    member_share, row_cells = state.shape
    chunks = len(parts)
    shares, _, sub, _ = parts[0].shape
    tile = min(512, row_cells)
    return pl.pallas_call(
        functools.partial(law_kernel, chunks),
        grid_spec=pltpu.PrefetchScalarGridSpec(
            num_scalar_prefetch=1,
            grid=(row_cells // tile,),
            in_specs=[pl.BlockSpec((shares, 3, sub, tile), lambda e, col: (0, 0, 0, e))] * chunks
            + [
                pl.BlockSpec((3, member_share, tile), lambda e, col: (0, col[0], e)),
                pl.BlockSpec((member_share, tile), lambda e, col: (0, e)),
                pl.BlockSpec((3, tile), lambda e, col: (0, e)),
            ],
            out_specs=pl.BlockSpec((3, member_share, tile), lambda e, col: (0, 0, e)),
        ),
        out_shape=jax.ShapeDtypeStruct((3, member_share, row_cells), jnp.float32),
        compiler_params=pltpu.CompilerParams(vmem_limit_bytes=24 * MIB),
        cost_estimate=pl.CostEstimate(flops=MIB * 16, bytes_accessed=8 * MIB, transcendentals=0),
        name="law",
    )(col, *parts, velocity, state, friction)


def shards(
    velocity,
    state,
    friction,
    near_src,
    near_block,
    far_dest,
    far_rank,
    far_basis_v,
    far_target,
    far_basis_u,
):
    members, _, row_cells = velocity.shape
    clusters = row_cells // CS
    near_count = near_src.shape[1]
    far_count = far_dest.shape[2]
    rank_width, width = far_basis_v.shape[3:]
    patches = lax.axis_size("patch")
    shares = lax.axis_size("col")
    capacity = far_target.shape[3]
    slots = patches * capacity
    member_share = state.shape[0]
    sub = member_share // CHUNKS
    planes = jnp.transpose(velocity, (1, 0, 2))
    split = planes.reshape(3, shares, CHUNKS, sub, row_cells)
    basis_v = far_basis_v.reshape(clusters, far_count * rank_width, width)
    basis_u = far_basis_u.reshape(slots, rank_width, width)
    blocks = near_block
    dest = far_dest.reshape(-1)
    rank = far_rank.reshape(-1)
    target = far_target.reshape(-1)
    first = lax.axis_index("patch") * clusters - clusters
    src = (near_src - first).reshape(-1)
    ends = patches - 1
    up = [(i, i + 1) for i in range(ends)]
    down = [(i + 1, i) for i in range(ends)]
    parts = []
    for h in range(CHUNKS):
        own, coef = source_step(h, split, basis_v, dest, rank)(slots)
        left = lax.ppermute(own, "patch", up)
        right = lax.ppermute(own, "patch", down)
        arrived = lax.all_to_all(coef, "patch", split_axis=0, concat_axis=0, tiled=True)
        partial = target_step(shares, src, target, left, own, right, blocks, arrived, basis_u)
        parts.append(lax.all_to_all(partial, "col", split_axis=0, concat_axis=0, tiled=True))
    col = lax.axis_index("col").reshape(1).astype(jnp.int32)
    rate = law_step(col, parts, planes, state, friction)
    return jnp.transpose(rate, (1, 0, 2))


def solution(mesh):
    return jax.shard_map(
        shards,
        mesh=mesh,
        in_specs=(
            P("runs", None, "patch"),
            P(("runs", "col"), "patch"),
            P("runs", "patch"),
            P("patch", "col"),
            P("patch", "col", None, None),
            P("col", "patch", None),
            P("col", "patch", None),
            P("col", "patch", None, None, None),
            P("col", "patch", None, None),
            P("col", "patch", None, None, None, None),
        ),
        out_specs=P(("runs", "col"), None, "patch"),
        check_vma=False,
    )
```

```python
import functools
import jax
import jax.numpy as jnp
from jax import lax
from jax.experimental import pallas as pl
from jax.experimental.pallas import tpu as pltpu
from jax.sharding import PartitionSpec as P

CS = 128
CHUNKS = 1
PIECES = 4
GROUP = 8
MIB = 1 << 20
MESH = pl.DeviceIdType.MESH

damping = 0.5
speed_floor = 0.25

NT = (((1,), (1,)), ((), ()))
TN = (((0,), (0,)), ((), ()))


def source_kernel(far_count, rank_width, dest_ref, rank_ref, vel_ref, basis_ref, own_ref, coef_ref):
    g = pl.program_id(0)
    members = own_ref.shape[1]
    for c in range(3):
        part = vel_ref[c].reshape(members, CS).astype(jnp.bfloat16)
        own_ref[0, :, c * CS : (c + 1) * CS] = part
    raw = lax.dot_general(basis_ref[0], own_ref[0], NT, preferred_element_type=jnp.float32)
    rows = lax.broadcasted_iota(jnp.int32, (rank_width, members), 0)
    for j in range(far_count):
        block = raw[j * rank_width : (j + 1) * rank_width]
        block = jnp.where(rows < rank_ref[g * far_count + j], block, 0.0)
        coef_ref[dest_ref[g * far_count + j]] = block.astype(jnp.bfloat16)


def source_step(chunk, velocity, basis_v, dest, rank):
    _, shares, _, sub, row_cells = velocity.shape
    members = shares * sub
    clusters = row_cells // CS
    far_count = dest.shape[0] // clusters
    rank_width = basis_v.shape[1] // far_count
    width = basis_v.shape[2]

    def call(slots):
        return pl.pallas_call(
            functools.partial(source_kernel, far_count, rank_width),
            grid_spec=pltpu.PrefetchScalarGridSpec(
                num_scalar_prefetch=2,
                grid=(clusters,),
                in_specs=[
                    pl.BlockSpec((3, shares, None, sub, CS), lambda g, *_: (0, 0, chunk, 0, g)),
                    pl.BlockSpec((1, far_count * rank_width, width), lambda g, *_: (g, 0, 0)),
                ],
                out_specs=[
                    pl.BlockSpec((1, members, width), lambda g, *_: (g, 0, 0)),
                    pl.BlockSpec((slots, rank_width, members), lambda g, *_: (0, 0, 0)),
                ],
            ),
            out_shape=[
                jax.ShapeDtypeStruct((clusters, members, width), jnp.bfloat16),
                jax.ShapeDtypeStruct((slots, rank_width, members), jnp.bfloat16),
            ],
            compiler_params=pltpu.CompilerParams(vmem_limit_bytes=24 * MIB),
            cost_estimate=pl.CostEstimate(
                flops=2 * clusters * far_count * rank_width * width * members,
                bytes_accessed=8 * MIB,
                transcendentals=0,
            ),
            name="source",
        )(dest, rank, velocity, basis_v)

    return call


def target_kernel(
    near_count, rank_width, src_ref, target_ref,
    mate_ref, own_ref, cross_ref, block_ref, coef_ref, basis_ref,
    out_ref, cells, acc, picked_c, picked_u, slot_list, slot_count, sems,
):
    t = pl.program_id(0)
    clusters = own_ref.shape[0]
    slots = coef_ref.shape[0]
    shares, _, sub, _ = out_ref.shape

    @pl.when(t == 0)
    def _():
        copies = [
            pltpu.make_async_copy(ref, cells.at[pl.ds(i * clusters, clusters)], sems.at[i])
            for i, ref in enumerate((mate_ref, own_ref, cross_ref))
        ]
        for copy in copies:
            copy.start()

        def clear(i, carry):
            slot_count[i] = 0
            return carry

        lax.fori_loop(0, clusters, clear, 0)

        def place(s, carry):
            goal = target_ref[s]

            @pl.when(goal >= 0)
            def _():
                at = slot_count[goal]
                slot_list[goal * slots + at] = s
                slot_count[goal] = at + 1

            return carry

        lax.fori_loop(0, slots, place, 0)
        for copy in copies:
            copy.wait()

    total = None
    for j in range(near_count):
        cell = cells[src_ref[t * near_count + j]]
        part = lax.dot_general(cell, block_ref[0, j], NT, preferred_element_type=jnp.float32)
        total = part if total is None else total + part
    acc[...] = total
    count = slot_count[t]

    def group(i, carry):
        for j in range(GROUP):
            at = i * GROUP + j
            live = at < count
            s = slot_list[t * slots + jnp.where(live, at, 0)]
            s = jnp.where(live, s, 0)
            piece = pl.ds(j * rank_width, rank_width)
            coef = coef_ref[s]
            picked_c[piece, :] = jnp.where(live, coef, jnp.zeros_like(coef))
            picked_u[piece, :] = basis_ref[s]
        acc[...] += lax.dot_general(
            picked_c[...], picked_u[...], TN, preferred_element_type=jnp.float32
        )
        return carry

    lax.fori_loop(0, (count + GROUP - 1) // GROUP, group, 0)
    for d in range(shares):
        for c in range(3):
            out_ref[d, c] = acc[d * sub : (d + 1) * sub, c * CS : (c + 1) * CS].astype(jnp.bfloat16)


def target_step(shares, src, target, mate, own, cross, blocks, coef, basis_u):
    clusters, members, width = own.shape
    near_count = blocks.shape[1]
    slots, rank_width, _ = coef.shape
    sub = members // shares
    whole = lambda t, *_: (0, 0, 0)
    return pl.pallas_call(
        functools.partial(target_kernel, near_count, rank_width),
        grid_spec=pltpu.PrefetchScalarGridSpec(
            num_scalar_prefetch=2,
            grid=(clusters,),
            in_specs=[
                pl.BlockSpec(memory_space=pl.ANY),
                pl.BlockSpec(memory_space=pl.ANY),
                pl.BlockSpec(memory_space=pl.ANY),
                pl.BlockSpec((1, near_count, width, width), lambda t, *_: (t, 0, 0, 0)),
                pl.BlockSpec((slots, rank_width, members), whole),
                pl.BlockSpec((slots, rank_width, width), whole),
            ],
            out_specs=pl.BlockSpec((shares, 3, sub, CS), lambda t, *_: (0, 0, 0, t)),
            scratch_shapes=[
                pltpu.VMEM((3 * clusters, members, width), jnp.bfloat16),
                pltpu.VMEM((members, width), jnp.float32),
                pltpu.VMEM((GROUP * rank_width, members), jnp.bfloat16),
                pltpu.VMEM((GROUP * rank_width, width), jnp.bfloat16),
                pltpu.SMEM((clusters * slots,), jnp.int32),
                pltpu.SMEM((clusters,), jnp.int32),
                pltpu.SemaphoreType.DMA((3,)),
            ],
        ),
        out_shape=jax.ShapeDtypeStruct((shares, 3, sub, clusters * CS), jnp.bfloat16),
        compiler_params=pltpu.CompilerParams(vmem_limit_bytes=36 * MIB),
        cost_estimate=pl.CostEstimate(
            flops=2 * clusters * members * width * (near_count * width + GROUP * rank_width),
            bytes_accessed=24 * MIB,
            transcendentals=0,
        ),
        name="target",
    )(src, target, mate, own, cross, blocks, coef, basis_u)


def law_kernel(chunks, col_ref, *refs):
    parts = refs[:chunks]
    vel_ref, state_ref, friction_ref, out_ref = refs[chunks:]
    sub = parts[0].shape[2]
    for h in range(chunks):
        rows = slice(h * sub, (h + 1) * sub)
        velocity = [vel_ref[c, rows, :] for c in range(3)]
        speed = jnp.sqrt(
            velocity[0] * velocity[0] + velocity[1] * velocity[1] + velocity[2] * velocity[2] + speed_floor
        )
        state = state_ref[rows, :]
        state_rate = 1.0 - speed * state / friction_ref[2:3, :]
        pulled = friction_ref[1:2, :] * state_rate / (state * speed)
        below = friction_ref[0:1, :] / speed + damping
        for c in range(3):
            stress = jnp.sum(parts[h][:, c].astype(jnp.float32), axis=0)
            out_ref[c, rows, :] = (-stress - pulled * velocity[c]) / below


def law_step(col, parts, velocity, state, friction):
    member_share, row_cells = state.shape
    chunks = len(parts)
    shares, _, sub, _ = parts[0].shape
    tile = min(512, row_cells)
    return pl.pallas_call(
        functools.partial(law_kernel, chunks),
        grid_spec=pltpu.PrefetchScalarGridSpec(
            num_scalar_prefetch=1,
            grid=(row_cells // tile,),
            in_specs=[pl.BlockSpec((shares, 3, sub, tile), lambda e, col: (0, 0, 0, e))] * chunks
            + [
                pl.BlockSpec((3, member_share, tile), lambda e, col: (0, col[0], e)),
                pl.BlockSpec((member_share, tile), lambda e, col: (0, e)),
                pl.BlockSpec((3, tile), lambda e, col: (0, e)),
            ],
            out_specs=pl.BlockSpec((3, member_share, tile), lambda e, col: (0, 0, e)),
        ),
        out_shape=jax.ShapeDtypeStruct((3, member_share, row_cells), jnp.float32),
        compiler_params=pltpu.CompilerParams(vmem_limit_bytes=24 * MIB),
        cost_estimate=pl.CostEstimate(flops=MIB * 16, bytes_accessed=8 * MIB, transcendentals=0),
        name="law",
    )(col, *parts, velocity, state, friction)


def remote(src, dst, send, recv, axis, peer):
    return pltpu.make_async_remote_copy(
        src_ref=src,
        dst_ref=dst,
        send_sem=send,
        recv_sem=recv,
        device_id={axis: peer},
        device_id_type=MESH,
    )


def exchange_kernel(
    patches, cols, own, coef, mate_out, cross_out, arrived,
    mate_sems, cross_send, cross_recv, share_send, share_recv, coef_send, coef_recv, local_sem,
):
    p = lax.axis_index("patch")
    c = lax.axis_index("col")
    odd = p % 2
    mate = p + 1 - 2 * odd
    cross = p + 2 * odd - 1
    crosses = jnp.logical_and(cross >= 0, cross < patches)
    per = own.shape[0] // cols
    capacity = coef.shape[0] // patches

    barrier = pltpu.get_barrier_semaphore()
    for j in range(1, patches):
        pl.semaphore_signal(barrier, inc=1, device_id={"patch": (p + j) % patches}, device_id_type=MESH)
    for j in range(1, cols):
        pl.semaphore_signal(barrier, inc=1, device_id={"col": (c + j) % cols}, device_id_type=MESH)
    pl.semaphore_wait(barrier, patches + cols - 2)

    def crossing(k):
        at = c * per + k
        return remote(own.at[at], cross_out.at[at], cross_send.at[k], cross_recv.at[k], "patch", cross)

    def share(j, k):
        at = c * per + k
        return remote(
            cross_out.at[at], cross_out.at[at], share_send.at[j - 1, k], share_recv.at[j - 1, k],
            "col", (c + j) % cols,
        )

    def shared(j, k):
        at = ((c + cols - j) % cols) * per + k
        return remote(
            cross_out.at[at], cross_out.at[at], share_send.at[j - 1, k], share_recv.at[j - 1, k],
            "col", (c + j) % cols,
        )

    def coefficients(j):
        q = (p + j) % patches
        return remote(
            coef.at[pl.ds(q * capacity, capacity)], arrived.at[pl.ds(p * capacity, capacity)],
            coef_send.at[j - 1], coef_recv.at[j - 1], "patch", q,
        )

    def coefficients_in(j):
        q = (p + patches - j) % patches
        return remote(
            coef.at[pl.ds(q * capacity, capacity)], arrived.at[pl.ds(q * capacity, capacity)],
            coef_send.at[j - 1], coef_recv.at[j - 1], "patch", (p + j) % patches,
        )

    @pl.when(crosses)
    def _():
        for k in range(per):
            crossing(k).start()

    for j in range(1, patches):
        coefficients(j).start()
    to_mate = remote(own, mate_out, mate_sems.at[0], mate_sems.at[1], "patch", mate)
    to_mate.start()
    kept = pl.ds(p * capacity, capacity)
    keep = pltpu.make_async_copy(coef.at[kept], arrived.at[kept], local_sem)
    keep.start()

    @pl.when(crosses)
    def _():
        for k in range(per):
            crossing(k).wait_recv()
            for j in range(1, cols):
                share(j, k).start()
        for k in range(per):
            for j in range(1, cols):
                shared(j, k).wait_recv()
        for k in range(per):
            crossing(k).wait_send()
            for j in range(1, cols):
                share(j, k).wait_send()

    keep.wait()
    to_mate.wait()
    for j in range(1, patches):
        coefficients_in(j).wait_recv()
        coefficients(j).wait_send()


def exchange_step(patches, cols, own, coef):
    per = own.shape[0] // cols
    dma = pltpu.SemaphoreType.DMA
    return pl.pallas_call(
        functools.partial(exchange_kernel, patches, cols),
        in_specs=[pl.BlockSpec(memory_space=pl.ANY)] * 2,
        out_specs=[pl.BlockSpec(memory_space=pl.ANY)] * 3,
        out_shape=[
            jax.ShapeDtypeStruct(own.shape, own.dtype),
            jax.ShapeDtypeStruct(own.shape, own.dtype),
            jax.ShapeDtypeStruct(coef.shape, coef.dtype),
        ],
        scratch_shapes=[
            dma((2,)),
            dma((per,)),
            dma((per,)),
            dma((cols - 1, per)),
            dma((cols - 1, per)),
            dma((patches - 1,)),
            dma((patches - 1,)),
            dma(()),
        ],
        compiler_params=pltpu.CompilerParams(
            collective_id=0, has_side_effects=True, vmem_limit_bytes=8 * MIB
        ),
        name="exchange",
    )(own, coef)


def line_kernel(
    cols, part_ref, out_ref, up_in, up_out, down_in, down_out,
    up_send, up_recv, down_send, down_recv,
):
    me = lax.axis_index("col")
    width = part_ref.shape[3] // PIECES
    not_first = me > 0
    not_last = me < cols - 1

    barrier = pltpu.get_barrier_semaphore()

    @pl.when(not_first)
    def _():
        pl.semaphore_signal(barrier, inc=1, device_id={"col": me - 1}, device_id_type=MESH)

    @pl.when(not_last)
    def _():
        pl.semaphore_signal(barrier, inc=1, device_id={"col": me + 1}, device_id_type=MESH)

    pl.semaphore_wait(barrier, jnp.where(jnp.logical_and(not_first, not_last), 2, 1))

    def span(k):
        return pl.ds(pl.multiple_of(k * width, width), width)

    def hop(up, d, k):
        out, into = (up_out, up_in) if up else (down_out, down_in)
        send, recv = (up_send, up_recv) if up else (down_send, down_recv)
        peer = me + 1 if up else me - 1
        piece = (d, slice(None), slice(None), span(k))
        return remote(out.at[piece], into.at[piece], send.at[d, k], recv.at[d, k], "col", peer)

    def step(up, d, k):
        out, into = (up_out, up_in) if up else (down_out, down_in)
        more = not_first if up else not_last
        piece = (d, slice(None), slice(None), span(k))

        @pl.when(more)
        def _():
            hop(up, d, k).wait_recv()
            total = part_ref[piece].astype(jnp.float32) + into[piece].astype(jnp.float32)
            out[piece] = total.astype(jnp.bfloat16)

        @pl.when(jnp.logical_not(more))
        def _():
            out[piece] = part_ref[piece]

        hop(up, d, k).start()

    count = (cols - 1) * PIECES
    up_first = me < cols - 1 - me

    def send_all(i, carry):
        j, k = i // PIECES, i % PIECES
        high, low = cols - 1 - j, j
        sends_up = high > me
        sends_down = low < me

        @pl.when(jnp.logical_and(sends_up, up_first))
        def _():
            step(True, high, k)

        @pl.when(sends_down)
        def _():
            step(False, low, k)

        @pl.when(jnp.logical_and(sends_up, jnp.logical_not(up_first)))
        def _():
            step(True, high, k)

        return carry

    lax.fori_loop(0, count, send_all, 0)

    def finish(k, carry):
        piece = (me, slice(None), slice(None), span(k))
        goal = (slice(None), slice(None), span(k))
        out_ref[goal] = part_ref[piece].astype(jnp.float32)

        @pl.when(not_first)
        def _():
            hop(True, me, k).wait_recv()
            out_ref[goal] += up_in[piece].astype(jnp.float32)

        @pl.when(not_last)
        def _():
            hop(False, me, k).wait_recv()
            out_ref[goal] += down_in[piece].astype(jnp.float32)

        return carry

    lax.fori_loop(0, PIECES, finish, 0)

    def settle(i, carry):
        j, k = i // PIECES, i % PIECES
        high, low = cols - 1 - j, j

        @pl.when(high > me)
        def _():
            hop(True, high, k).wait_send()

        @pl.when(low < me)
        def _():
            hop(False, low, k).wait_send()

        return carry

    lax.fori_loop(0, count, settle, 0)


def line_step(partial):
    cols, _, sub, row_cells = partial.shape
    dma = pltpu.SemaphoreType.DMA
    return pl.pallas_call(
        functools.partial(line_kernel, cols),
        in_specs=[pl.BlockSpec(memory_space=pltpu.VMEM)],
        out_specs=pl.BlockSpec(memory_space=pltpu.VMEM),
        out_shape=jax.ShapeDtypeStruct((3, sub, row_cells), jnp.float32),
        scratch_shapes=[pltpu.VMEM(partial.shape, jnp.bfloat16)] * 4 + [dma((cols, PIECES))] * 4,
        compiler_params=pltpu.CompilerParams(
            collective_id=1, has_side_effects=True, vmem_limit_bytes=32 * MIB
        ),
        name="line",
    )(partial)


def shards(
    velocity,
    state,
    friction,
    near_src,
    near_block,
    far_dest,
    far_rank,
    far_basis_v,
    far_target,
    far_basis_u,
):
    members, _, row_cells = velocity.shape
    clusters = row_cells // CS
    near_count = near_src.shape[1]
    far_count = far_dest.shape[2]
    rank_width, width = far_basis_v.shape[3:]
    patches = lax.axis_size("patch")
    shares = lax.axis_size("col")
    capacity = far_target.shape[3]
    slots = patches * capacity
    member_share = state.shape[0]
    sub = member_share // CHUNKS
    planes = jnp.transpose(velocity, (1, 0, 2))
    split = planes.reshape(3, shares, CHUNKS, sub, row_cells)
    basis_v = far_basis_v.reshape(clusters, far_count * rank_width, width)
    basis_u = far_basis_u.reshape(slots, rank_width, width)
    blocks = near_block
    dest = far_dest.reshape(-1)
    rank = far_rank.reshape(-1)
    target = far_target.reshape(-1)
    at_patch = lax.axis_index("patch")
    offset = near_src - (at_patch - 1) * clusters
    row, cell = offset // clusters, offset % clusters
    row = jnp.where(at_patch % 2 == 0, 2 - row, row)
    src = (row * clusters + cell).reshape(-1)
    own, coef = source_step(0, split, basis_v, dest, rank)(slots)
    mate, cross, arrived = exchange_step(patches, shares, own, coef)
    partial = target_step(shares, src, target, mate, own, cross, blocks, arrived, basis_u)
    parts = [line_step(partial)[None]]
    col = lax.axis_index("col").reshape(1).astype(jnp.int32)
    rate = law_step(col, parts, planes, state, friction)
    return jnp.transpose(rate, (1, 0, 2))


def solution(mesh):
    return jax.shard_map(
        shards,
        mesh=mesh,
        in_specs=(
            P("runs", None, "patch"),
            P(("runs", "col"), "patch"),
            P("runs", "patch"),
            P("patch", "col"),
            P("patch", "col", None, None),
            P("col", "patch", None),
            P("col", "patch", None),
            P("col", "patch", None, None, None),
            P("col", "patch", None, None),
            P("col", "patch", None, None, None, None),
        ),
        out_specs=P(("runs", "col"), None, "patch"),
        check_vma=False,
    )
```

```python
import functools
import jax
import jax.numpy as jnp
from jax import lax
from jax.experimental import pallas as pl
from jax.experimental.pallas import tpu as pltpu
from jax.sharding import PartitionSpec as P

CS = 128
CHUNKS = 1
PIECES = 4
GROUP = 8
MIB = 1 << 20
MESH = pl.DeviceIdType.MESH

damping = 0.5
speed_floor = 0.25

NT = (((1,), (1,)), ((), ()))
TN = (((0,), (0,)), ((), ()))


def source_kernel(far_count, rank_width, dest_ref, rank_ref, vel_ref, basis_ref, own_ref, coef_ref):
    g = pl.program_id(0)
    members = own_ref.shape[1]
    for c in range(3):
        part = vel_ref[c].reshape(members, CS).astype(jnp.bfloat16)
        own_ref[0, :, c * CS : (c + 1) * CS] = part
    raw = lax.dot_general(basis_ref[0], own_ref[0], NT, preferred_element_type=jnp.float32)
    rows = lax.broadcasted_iota(jnp.int32, (rank_width, members), 0)
    for j in range(far_count):
        block = raw[j * rank_width : (j + 1) * rank_width]
        block = jnp.where(rows < rank_ref[g * far_count + j], block, 0.0)
        coef_ref[dest_ref[g * far_count + j]] = block.astype(jnp.bfloat16)


def source_step(chunk, velocity, basis_v, dest, rank):
    _, shares, _, sub, row_cells = velocity.shape
    members = shares * sub
    clusters = row_cells // CS
    far_count = dest.shape[0] // clusters
    rank_width = basis_v.shape[1] // far_count
    width = basis_v.shape[2]

    def call(slots):
        return pl.pallas_call(
            functools.partial(source_kernel, far_count, rank_width),
            grid_spec=pltpu.PrefetchScalarGridSpec(
                num_scalar_prefetch=2,
                grid=(clusters,),
                in_specs=[
                    pl.BlockSpec((3, shares, None, sub, CS), lambda g, *_: (0, 0, chunk, 0, g)),
                    pl.BlockSpec((1, far_count * rank_width, width), lambda g, *_: (g, 0, 0)),
                ],
                out_specs=[
                    pl.BlockSpec((1, members, width), lambda g, *_: (g, 0, 0)),
                    pl.BlockSpec((slots, rank_width, members), lambda g, *_: (0, 0, 0)),
                ],
            ),
            out_shape=[
                jax.ShapeDtypeStruct((clusters, members, width), jnp.bfloat16),
                jax.ShapeDtypeStruct((slots, rank_width, members), jnp.bfloat16),
            ],
            compiler_params=pltpu.CompilerParams(vmem_limit_bytes=24 * MIB),
            cost_estimate=pl.CostEstimate(
                flops=2 * clusters * far_count * rank_width * width * members,
                bytes_accessed=8 * MIB,
                transcendentals=0,
            ),
            name="source",
        )(dest, rank, velocity, basis_v)

    return call


def target_kernel(
    near_count, rank_width, src_ref, target_ref,
    cells, block_ref, coef_ref, basis_ref,
    out_ref, acc, picked_c, picked_u, slot_list, slot_count,
):
    t = pl.program_id(0)
    clusters = cells.shape[0] // 3
    slots = coef_ref.shape[0]
    shares, _, sub, _ = out_ref.shape

    @pl.when(t == 0)
    def _():
        def clear(i, carry):
            slot_count[i] = 0
            return carry

        lax.fori_loop(0, clusters, clear, 0)

        def place(s, carry):
            goal = target_ref[s]

            @pl.when(goal >= 0)
            def _():
                at = slot_count[goal]
                slot_list[goal * slots + at] = s
                slot_count[goal] = at + 1

            return carry

        lax.fori_loop(0, slots, place, 0)

    total = None
    for j in range(near_count):
        cell = cells[src_ref[t * near_count + j]]
        part = lax.dot_general(cell, block_ref[0, j], NT, preferred_element_type=jnp.float32)
        total = part if total is None else total + part
    acc[...] = total
    count = slot_count[t]

    def group(i, carry):
        for j in range(GROUP):
            at = i * GROUP + j
            live = at < count
            s = slot_list[t * slots + jnp.where(live, at, 0)]
            s = jnp.where(live, s, 0)
            piece = pl.ds(j * rank_width, rank_width)
            coef = coef_ref[s]
            picked_c[piece, :] = jnp.where(live, coef, jnp.zeros_like(coef))
            picked_u[piece, :] = basis_ref[s]
        acc[...] += lax.dot_general(
            picked_c[...], picked_u[...], TN, preferred_element_type=jnp.float32
        )
        return carry

    lax.fori_loop(0, (count + GROUP - 1) // GROUP, group, 0)
    for d in range(shares):
        for c in range(3):
            out_ref[d, c] = acc[d * sub : (d + 1) * sub, c * CS : (c + 1) * CS].astype(jnp.bfloat16)


def target_step(shares, src, target, cells, blocks, coef, basis_u):
    clusters = cells.shape[0] // 3
    _, members, width = cells.shape
    near_count = blocks.shape[1]
    slots, rank_width, _ = coef.shape
    sub = members // shares
    return pl.pallas_call(
        functools.partial(target_kernel, near_count, rank_width),
        grid_spec=pltpu.PrefetchScalarGridSpec(
            num_scalar_prefetch=2,
            grid=(clusters,),
            in_specs=[
                pl.BlockSpec(memory_space=pltpu.VMEM),
                pl.BlockSpec((1, near_count, width, width), lambda t, *_: (t, 0, 0, 0)),
                pl.BlockSpec(memory_space=pltpu.VMEM),
                pl.BlockSpec(memory_space=pltpu.VMEM),
            ],
            out_specs=pl.BlockSpec((shares, 3, sub, CS), lambda t, *_: (0, 0, 0, t)),
            scratch_shapes=[
                pltpu.VMEM((members, width), jnp.float32),
                pltpu.VMEM((GROUP * rank_width, members), jnp.bfloat16),
                pltpu.VMEM((GROUP * rank_width, width), jnp.bfloat16),
                pltpu.SMEM((clusters * slots,), jnp.int32),
                pltpu.SMEM((clusters,), jnp.int32),
            ],
        ),
        out_shape=jax.ShapeDtypeStruct((shares, 3, sub, clusters * CS), jnp.bfloat16),
        compiler_params=pltpu.CompilerParams(vmem_limit_bytes=34 * MIB),
        cost_estimate=pl.CostEstimate(
            flops=2 * clusters * members * width * (near_count * width + GROUP * rank_width),
            bytes_accessed=24 * MIB,
            transcendentals=0,
        ),
        name="target",
    )(src, target, cells, blocks, coef, basis_u)


def law_kernel(chunks, col_ref, *refs):
    parts = refs[:chunks]
    vel_ref, state_ref, friction_ref, out_ref = refs[chunks:]
    sub = parts[0].shape[2]
    for h in range(chunks):
        rows = slice(h * sub, (h + 1) * sub)
        velocity = [vel_ref[c, rows, :] for c in range(3)]
        speed = jnp.sqrt(
            velocity[0] * velocity[0] + velocity[1] * velocity[1] + velocity[2] * velocity[2] + speed_floor
        )
        state = state_ref[rows, :]
        state_rate = 1.0 - speed * state / friction_ref[2:3, :]
        pulled = friction_ref[1:2, :] * state_rate / (state * speed)
        below = friction_ref[0:1, :] / speed + damping
        for c in range(3):
            stress = jnp.sum(parts[h][:, c].astype(jnp.float32), axis=0)
            out_ref[c, rows, :] = (-stress - pulled * velocity[c]) / below


def law_step(col, parts, velocity, state, friction):
    member_share, row_cells = state.shape
    chunks = len(parts)
    shares, _, sub, _ = parts[0].shape
    tile = min(512, row_cells)
    return pl.pallas_call(
        functools.partial(law_kernel, chunks),
        grid_spec=pltpu.PrefetchScalarGridSpec(
            num_scalar_prefetch=1,
            grid=(row_cells // tile,),
            in_specs=[pl.BlockSpec((shares, 3, sub, tile), lambda e, col: (0, 0, 0, e))] * chunks
            + [
                pl.BlockSpec((3, member_share, tile), lambda e, col: (0, col[0], e)),
                pl.BlockSpec((member_share, tile), lambda e, col: (0, e)),
                pl.BlockSpec((3, tile), lambda e, col: (0, e)),
            ],
            out_specs=pl.BlockSpec((3, member_share, tile), lambda e, col: (0, 0, e)),
        ),
        out_shape=jax.ShapeDtypeStruct((3, member_share, row_cells), jnp.float32),
        compiler_params=pltpu.CompilerParams(vmem_limit_bytes=24 * MIB),
        cost_estimate=pl.CostEstimate(flops=MIB * 16, bytes_accessed=8 * MIB, transcendentals=0),
        name="law",
    )(col, *parts, velocity, state, friction)


def remote(src, dst, send, recv, axis, peer):
    return pltpu.make_async_remote_copy(
        src_ref=src,
        dst_ref=dst,
        send_sem=send,
        recv_sem=recv,
        device_id={axis: peer},
        device_id_type=MESH,
    )


def exchange_kernel(
    patches, cols, own, coef, cells, arrived,
    mate_sems, cross_send, cross_recv, share_send, share_recv, coef_send, coef_recv, local_sems,
):
    p = lax.axis_index("patch")
    c = lax.axis_index("col")
    odd = p % 2
    mate = p + 1 - 2 * odd
    cross = p + 2 * odd - 1
    crosses = jnp.logical_and(cross >= 0, cross < patches)
    per = own.shape[0] // cols
    capacity = coef.shape[0] // patches

    clusters = own.shape[0]
    mate_out = cells.at[pl.ds(0, clusters)]
    own_out = cells.at[pl.ds(clusters, clusters)]
    cross_at = 2 * clusters
    place = pltpu.make_async_copy(own, own_out, local_sems.at[1])
    barrier = pltpu.get_barrier_semaphore()
    for j in range(1, patches):
        pl.semaphore_signal(barrier, inc=1, device_id={"patch": (p + j) % patches}, device_id_type=MESH)
    for j in range(1, cols):
        pl.semaphore_signal(barrier, inc=1, device_id={"col": (c + j) % cols}, device_id_type=MESH)
    pl.semaphore_wait(barrier, patches + cols - 2)

    def crossing(k):
        at = c * per + k
        return remote(own.at[at], cells.at[cross_at + at], cross_send.at[k], cross_recv.at[k], "patch", cross)

    def share(j, k):
        at = c * per + k
        return remote(
            cells.at[cross_at + at], cells.at[cross_at + at], share_send.at[j - 1, k], share_recv.at[j - 1, k],
            "col", (c + j) % cols,
        )

    def shared(j, k):
        at = ((c + cols - j) % cols) * per + k
        return remote(
            cells.at[cross_at + at], cells.at[cross_at + at], share_send.at[j - 1, k], share_recv.at[j - 1, k],
            "col", (c + j) % cols,
        )

    def coefficients(j):
        q = (p + j) % patches
        return remote(
            coef.at[pl.ds(q * capacity, capacity)], arrived.at[pl.ds(p * capacity, capacity)],
            coef_send.at[j - 1], coef_recv.at[j - 1], "patch", q,
        )

    def coefficients_in(j):
        q = (p + patches - j) % patches
        return remote(
            coef.at[pl.ds(q * capacity, capacity)], arrived.at[pl.ds(q * capacity, capacity)],
            coef_send.at[j - 1], coef_recv.at[j - 1], "patch", (p + j) % patches,
        )

    to_mate = remote(own, mate_out, mate_sems.at[0], mate_sems.at[1], "patch", mate)
    kept = pl.ds(p * capacity, capacity)
    keep = pltpu.make_async_copy(coef.at[kept], arrived.at[kept], local_sems.at[0])

    @pl.when(crosses)
    def _():
        for k in range(per):
            crossing(k).start()

    to_mate.start()
    keep.start()
    place.start()

    @pl.when(crosses)
    def _():
        for k in range(per):
            crossing(k).wait_recv()
            for j in range(1, cols):
                share(j, k).start()

    to_mate.wait_recv()
    for j in range(1, patches):
        coefficients(j).start()

    @pl.when(crosses)
    def _():
        for k in range(per):
            for j in range(1, cols):
                shared(j, k).wait_recv()
        for k in range(per):
            crossing(k).wait_send()
            for j in range(1, cols):
                share(j, k).wait_send()

    keep.wait()
    place.wait()
    to_mate.wait_send()
    for j in range(1, patches):
        coefficients_in(j).wait_recv()
        coefficients(j).wait_send()


def exchange_step(patches, cols, own, coef):
    per = own.shape[0] // cols
    dma = pltpu.SemaphoreType.DMA
    return pl.pallas_call(
        functools.partial(exchange_kernel, patches, cols),
        in_specs=[pl.BlockSpec(memory_space=pltpu.VMEM)] * 2,
        out_specs=[pl.BlockSpec(memory_space=pltpu.VMEM)] * 2,
        out_shape=[
            jax.ShapeDtypeStruct((3 * own.shape[0],) + own.shape[1:], own.dtype),
            jax.ShapeDtypeStruct(coef.shape, coef.dtype),
        ],
        scratch_shapes=[
            dma((2,)),
            dma((per,)),
            dma((per,)),
            dma((cols - 1, per)),
            dma((cols - 1, per)),
            dma((patches - 1,)),
            dma((patches - 1,)),
            dma((2,)),
        ],
        compiler_params=pltpu.CompilerParams(
            collective_id=0, has_side_effects=True, vmem_limit_bytes=8 * MIB
        ),
        name="exchange",
    )(own, coef)


def line_kernel(
    cols, part_ref, out_ref, up_in, up_out, down_in, down_out,
    up_send, up_recv, down_send, down_recv,
):
    me = lax.axis_index("col")
    width = part_ref.shape[3] // PIECES
    not_first = me > 0
    not_last = me < cols - 1

    barrier = pltpu.get_barrier_semaphore()

    @pl.when(not_first)
    def _():
        pl.semaphore_signal(barrier, inc=1, device_id={"col": me - 1}, device_id_type=MESH)

    @pl.when(not_last)
    def _():
        pl.semaphore_signal(barrier, inc=1, device_id={"col": me + 1}, device_id_type=MESH)

    pl.semaphore_wait(barrier, jnp.where(jnp.logical_and(not_first, not_last), 2, 1))

    def span(k):
        return pl.ds(pl.multiple_of(k * width, width), width)

    def hop(up, d, k):
        out, into = (up_out, up_in) if up else (down_out, down_in)
        send, recv = (up_send, up_recv) if up else (down_send, down_recv)
        peer = me + 1 if up else me - 1
        piece = (d, slice(None), slice(None), span(k))
        return remote(out.at[piece], into.at[piece], send.at[d, k], recv.at[d, k], "col", peer)

    def step(up, d, k):
        out, into = (up_out, up_in) if up else (down_out, down_in)
        more = not_first if up else not_last
        piece = (d, slice(None), slice(None), span(k))

        @pl.when(more)
        def _():
            hop(up, d, k).wait_recv()
            total = part_ref[piece].astype(jnp.float32) + into[piece].astype(jnp.float32)
            out[piece] = total.astype(jnp.bfloat16)

        @pl.when(jnp.logical_not(more))
        def _():
            out[piece] = part_ref[piece]

        hop(up, d, k).start()

    count = (cols - 1) * PIECES
    up_first = me < cols - 1 - me

    def send_all(i, carry):
        j, k = i // PIECES, i % PIECES
        high, low = cols - 1 - j, j
        sends_up = high > me
        sends_down = low < me

        @pl.when(jnp.logical_and(sends_up, up_first))
        def _():
            step(True, high, k)

        @pl.when(sends_down)
        def _():
            step(False, low, k)

        @pl.when(jnp.logical_and(sends_up, jnp.logical_not(up_first)))
        def _():
            step(True, high, k)

        return carry

    lax.fori_loop(0, count, send_all, 0)

    def finish(k, carry):
        piece = (me, slice(None), slice(None), span(k))
        goal = (slice(None), slice(None), span(k))
        out_ref[goal] = part_ref[piece].astype(jnp.float32)

        @pl.when(not_first)
        def _():
            hop(True, me, k).wait_recv()
            out_ref[goal] += up_in[piece].astype(jnp.float32)

        @pl.when(not_last)
        def _():
            hop(False, me, k).wait_recv()
            out_ref[goal] += down_in[piece].astype(jnp.float32)

        return carry

    lax.fori_loop(0, PIECES, finish, 0)

    def settle(i, carry):
        j, k = i // PIECES, i % PIECES
        high, low = cols - 1 - j, j

        @pl.when(high > me)
        def _():
            hop(True, high, k).wait_send()

        @pl.when(low < me)
        def _():
            hop(False, low, k).wait_send()

        return carry

    lax.fori_loop(0, count, settle, 0)


def line_step(partial):
    cols, _, sub, row_cells = partial.shape
    dma = pltpu.SemaphoreType.DMA
    return pl.pallas_call(
        functools.partial(line_kernel, cols),
        in_specs=[pl.BlockSpec(memory_space=pltpu.VMEM)],
        out_specs=pl.BlockSpec(memory_space=pltpu.VMEM),
        out_shape=jax.ShapeDtypeStruct((3, sub, row_cells), jnp.float32),
        scratch_shapes=[pltpu.VMEM(partial.shape, jnp.bfloat16)] * 4 + [dma((cols, PIECES))] * 4,
        compiler_params=pltpu.CompilerParams(
            collective_id=1, has_side_effects=True, vmem_limit_bytes=32 * MIB
        ),
        name="line",
    )(partial)


def shards(
    velocity,
    state,
    friction,
    near_src,
    near_block,
    far_dest,
    far_rank,
    far_basis_v,
    far_target,
    far_basis_u,
):
    members, _, row_cells = velocity.shape
    clusters = row_cells // CS
    near_count = near_src.shape[1]
    far_count = far_dest.shape[2]
    rank_width, width = far_basis_v.shape[3:]
    patches = lax.axis_size("patch")
    shares = lax.axis_size("col")
    capacity = far_target.shape[3]
    slots = patches * capacity
    member_share = state.shape[0]
    sub = member_share // CHUNKS
    planes = jnp.transpose(velocity, (1, 0, 2))
    split = planes.reshape(3, shares, CHUNKS, sub, row_cells)
    basis_v = far_basis_v.reshape(clusters, far_count * rank_width, width)
    basis_u = far_basis_u.reshape(slots, rank_width, width)
    blocks = near_block
    dest = far_dest.reshape(-1)
    rank = far_rank.reshape(-1)
    target = far_target.reshape(-1)
    at_patch = lax.axis_index("patch")
    offset = near_src - (at_patch - 1) * clusters
    row, cell = offset // clusters, offset % clusters
    row = jnp.where(at_patch % 2 == 0, 2 - row, row)
    src = (row * clusters + cell).reshape(-1)
    own, coef = source_step(0, split, basis_v, dest, rank)(slots)
    cells, arrived = exchange_step(patches, shares, own, coef)
    partial = target_step(shares, src, target, cells, blocks, arrived, basis_u)
    parts = [line_step(partial)[None]]
    col = lax.axis_index("col").reshape(1).astype(jnp.int32)
    rate = law_step(col, parts, planes, state, friction)
    return jnp.transpose(rate, (1, 0, 2))


def solution(mesh):
    return jax.shard_map(
        shards,
        mesh=mesh,
        in_specs=(
            P("runs", None, "patch"),
            P(("runs", "col"), "patch"),
            P("runs", "patch"),
            P("patch", "col"),
            P("patch", "col", None, None),
            P("col", "patch", None),
            P("col", "patch", None),
            P("col", "patch", None, None, None),
            P("col", "patch", None, None),
            P("col", "patch", None, None, None, None),
        ),
        out_specs=P(("runs", "col"), None, "patch"),
        check_vma=False,
    )
```

```python
import functools
import jax
import jax.numpy as jnp
from jax import lax
from jax.experimental import pallas as pl
from jax.experimental.pallas import tpu as pltpu
from jax.sharding import PartitionSpec as P

CS = 128
CHUNKS = 1
PIECES = 8
GROUP = 8
MIB = 1 << 20
MESH = pl.DeviceIdType.MESH

damping = 0.5
speed_floor = 0.25

NT = (((1,), (1,)), ((), ()))
TN = (((0,), (0,)), ((), ()))


def source_kernel(far_count, rank_width, dest_ref, rank_ref, vel_ref, basis_ref, own_ref, coef_ref):
    g = pl.program_id(0)
    members = own_ref.shape[1]
    for c in range(3):
        part = vel_ref[c].reshape(members, CS).astype(jnp.bfloat16)
        own_ref[0, :, c * CS : (c + 1) * CS] = part
    raw = lax.dot_general(basis_ref[0], own_ref[0], NT, preferred_element_type=jnp.float32)
    rows = lax.broadcasted_iota(jnp.int32, (rank_width, members), 0)
    for j in range(far_count):
        block = raw[j * rank_width : (j + 1) * rank_width]
        block = jnp.where(rows < rank_ref[g * far_count + j], block, 0.0)
        coef_ref[dest_ref[g * far_count + j]] = block.astype(jnp.bfloat16)


def source_step(chunk, velocity, basis_v, dest, rank):
    _, shares, _, sub, row_cells = velocity.shape
    members = shares * sub
    clusters = row_cells // CS
    far_count = dest.shape[0] // clusters
    rank_width = basis_v.shape[1] // far_count
    width = basis_v.shape[2]

    def call(slots):
        return pl.pallas_call(
            functools.partial(source_kernel, far_count, rank_width),
            grid_spec=pltpu.PrefetchScalarGridSpec(
                num_scalar_prefetch=2,
                grid=(clusters,),
                in_specs=[
                    pl.BlockSpec((3, shares, None, sub, CS), lambda g, *_: (0, 0, chunk, 0, g)),
                    pl.BlockSpec((1, far_count * rank_width, width), lambda g, *_: (g, 0, 0)),
                ],
                out_specs=[
                    pl.BlockSpec((1, members, width), lambda g, *_: (g, 0, 0)),
                    pl.BlockSpec((slots, rank_width, members), lambda g, *_: (0, 0, 0)),
                ],
            ),
            out_shape=[
                jax.ShapeDtypeStruct((clusters, members, width), jnp.bfloat16),
                jax.ShapeDtypeStruct((slots, rank_width, members), jnp.bfloat16),
            ],
            compiler_params=pltpu.CompilerParams(vmem_limit_bytes=24 * MIB),
            cost_estimate=pl.CostEstimate(
                flops=2 * clusters * far_count * rank_width * width * members,
                bytes_accessed=8 * MIB,
                transcendentals=0,
            ),
            name="source",
        )(dest, rank, velocity, basis_v)

    return call


def target_kernel(
    near_count, rank_width, src_ref, target_ref,
    mate_ref, own_ref, cross_ref, block_ref, coef_ref, basis_ref,
    out_ref, cells, acc, picked_c, picked_u, slot_list, slot_count, sems,
):
    t = pl.program_id(0)
    clusters = own_ref.shape[0]
    slots = coef_ref.shape[0]
    shares, _, sub, _ = out_ref.shape

    @pl.when(t == 0)
    def _():
        copies = [
            pltpu.make_async_copy(ref, cells.at[pl.ds(i * clusters, clusters)], sems.at[i])
            for i, ref in enumerate((mate_ref, own_ref, cross_ref))
        ]
        for copy in copies:
            copy.start()

        def clear(i, carry):
            slot_count[i] = 0
            return carry

        lax.fori_loop(0, clusters, clear, 0)

        def place(s, carry):
            goal = target_ref[s]

            @pl.when(goal >= 0)
            def _():
                at = slot_count[goal]
                slot_list[goal * slots + at] = s
                slot_count[goal] = at + 1

            return carry

        lax.fori_loop(0, slots, place, 0)
        for copy in copies:
            copy.wait()

    total = None
    for j in range(near_count):
        cell = cells[src_ref[t * near_count + j]]
        part = lax.dot_general(cell, block_ref[0, j], NT, preferred_element_type=jnp.float32)
        total = part if total is None else total + part
    acc[...] = total
    count = slot_count[t]

    def group(i, carry):
        for j in range(GROUP):
            at = i * GROUP + j
            live = at < count
            s = slot_list[t * slots + jnp.where(live, at, 0)]
            s = jnp.where(live, s, 0)
            piece = pl.ds(j * rank_width, rank_width)
            coef = coef_ref[s]
            picked_c[piece, :] = jnp.where(live, coef, jnp.zeros_like(coef))
            picked_u[piece, :] = basis_ref[s]
        acc[...] += lax.dot_general(
            picked_c[...], picked_u[...], TN, preferred_element_type=jnp.float32
        )
        return carry

    lax.fori_loop(0, (count + GROUP - 1) // GROUP, group, 0)
    for d in range(shares):
        for c in range(3):
            out_ref[d, c] = acc[d * sub : (d + 1) * sub, c * CS : (c + 1) * CS].astype(jnp.bfloat16)


def target_step(shares, src, target, mate, own, cross, blocks, coef, basis_u):
    clusters, members, width = own.shape
    near_count = blocks.shape[1]
    slots, rank_width, _ = coef.shape
    sub = members // shares
    whole = lambda t, *_: (0, 0, 0)
    return pl.pallas_call(
        functools.partial(target_kernel, near_count, rank_width),
        grid_spec=pltpu.PrefetchScalarGridSpec(
            num_scalar_prefetch=2,
            grid=(clusters,),
            in_specs=[
                pl.BlockSpec(memory_space=pl.ANY),
                pl.BlockSpec(memory_space=pl.ANY),
                pl.BlockSpec(memory_space=pl.ANY),
                pl.BlockSpec((1, near_count, width, width), lambda t, *_: (t, 0, 0, 0)),
                pl.BlockSpec((slots, rank_width, members), whole),
                pl.BlockSpec((slots, rank_width, width), whole),
            ],
            out_specs=pl.BlockSpec((shares, 3, sub, CS), lambda t, *_: (0, 0, 0, t)),
            scratch_shapes=[
                pltpu.VMEM((3 * clusters, members, width), jnp.bfloat16),
                pltpu.VMEM((members, width), jnp.float32),
                pltpu.VMEM((GROUP * rank_width, members), jnp.bfloat16),
                pltpu.VMEM((GROUP * rank_width, width), jnp.bfloat16),
                pltpu.SMEM((clusters * slots,), jnp.int32),
                pltpu.SMEM((clusters,), jnp.int32),
                pltpu.SemaphoreType.DMA((3,)),
            ],
        ),
        out_shape=jax.ShapeDtypeStruct((shares, 3, sub, clusters * CS), jnp.bfloat16),
        compiler_params=pltpu.CompilerParams(vmem_limit_bytes=36 * MIB),
        cost_estimate=pl.CostEstimate(
            flops=2 * clusters * members * width * (near_count * width + GROUP * rank_width),
            bytes_accessed=24 * MIB,
            transcendentals=0,
        ),
        name="target",
    )(src, target, mate, own, cross, blocks, coef, basis_u)


def law_kernel(chunks, col_ref, *refs):
    parts = refs[:chunks]
    vel_ref, state_ref, friction_ref, out_ref = refs[chunks:]
    sub = parts[0].shape[2]
    for h in range(chunks):
        rows = slice(h * sub, (h + 1) * sub)
        velocity = [vel_ref[c, rows, :] for c in range(3)]
        speed = jnp.sqrt(
            velocity[0] * velocity[0] + velocity[1] * velocity[1] + velocity[2] * velocity[2] + speed_floor
        )
        state = state_ref[rows, :]
        state_rate = 1.0 - speed * state / friction_ref[2:3, :]
        pulled = friction_ref[1:2, :] * state_rate / (state * speed)
        below = friction_ref[0:1, :] / speed + damping
        for c in range(3):
            stress = jnp.sum(parts[h][:, c].astype(jnp.float32), axis=0)
            out_ref[c, rows, :] = (-stress - pulled * velocity[c]) / below


def law_step(col, parts, velocity, state, friction):
    member_share, row_cells = state.shape
    chunks = len(parts)
    shares, _, sub, _ = parts[0].shape
    tile = min(512, row_cells)
    return pl.pallas_call(
        functools.partial(law_kernel, chunks),
        grid_spec=pltpu.PrefetchScalarGridSpec(
            num_scalar_prefetch=1,
            grid=(row_cells // tile,),
            in_specs=[pl.BlockSpec((shares, 3, sub, tile), lambda e, col: (0, 0, 0, e))] * chunks
            + [
                pl.BlockSpec((3, member_share, tile), lambda e, col: (0, col[0], e)),
                pl.BlockSpec((member_share, tile), lambda e, col: (0, e)),
                pl.BlockSpec((3, tile), lambda e, col: (0, e)),
            ],
            out_specs=pl.BlockSpec((3, member_share, tile), lambda e, col: (0, 0, e)),
        ),
        out_shape=jax.ShapeDtypeStruct((3, member_share, row_cells), jnp.float32),
        compiler_params=pltpu.CompilerParams(vmem_limit_bytes=24 * MIB),
        cost_estimate=pl.CostEstimate(flops=MIB * 16, bytes_accessed=8 * MIB, transcendentals=0),
        name="law",
    )(col, *parts, velocity, state, friction)


def remote(src, dst, send, recv, axis, peer):
    return pltpu.make_async_remote_copy(
        src_ref=src,
        dst_ref=dst,
        send_sem=send,
        recv_sem=recv,
        device_id={axis: peer},
        device_id_type=MESH,
    )


def exchange_kernel(
    patches, cols, own, coef, mate_out, cross_out, arrived,
    mate_sems, cross_send, cross_recv, up_send, down_send, share_recv, coef_send, coef_recv, local_sem,
):
    p = lax.axis_index("patch")
    c = lax.axis_index("col")
    odd = p % 2
    mate = p + 1 - 2 * odd
    cross = p + 2 * odd - 1
    crosses = jnp.logical_and(cross >= 0, cross < patches)
    per = own.shape[0] // cols
    capacity = coef.shape[0] // patches

    barrier = pltpu.get_barrier_semaphore()
    for j in range(1, patches):
        pl.semaphore_signal(barrier, inc=1, device_id={"patch": (p + j) % patches}, device_id_type=MESH)
    for j in range(1, cols):
        pl.semaphore_signal(barrier, inc=1, device_id={"col": (c + j) % cols}, device_id_type=MESH)
    pl.semaphore_wait(barrier, patches + cols - 2)

    def crossing(k):
        at = c * per + k
        return remote(own.at[at], cross_out.at[at], cross_send.at[k], cross_recv.at[k], "patch", cross)

    def pass_on(up, source, k):
        at = source * per + k
        send = up_send if up else down_send
        peer = c + 1 if up else c - 1
        return remote(
            cross_out.at[at], cross_out.at[at], send.at[source, k], share_recv.at[source, k], "col", peer
        )

    not_first = c > 0
    not_last = c < cols - 1

    def coefficients(j):
        q = (p + j) % patches
        return remote(
            coef.at[pl.ds(q * capacity, capacity)], arrived.at[pl.ds(p * capacity, capacity)],
            coef_send.at[j - 1], coef_recv.at[j - 1], "patch", q,
        )

    def coefficients_in(j):
        q = (p + patches - j) % patches
        return remote(
            coef.at[pl.ds(q * capacity, capacity)], arrived.at[pl.ds(q * capacity, capacity)],
            coef_send.at[j - 1], coef_recv.at[j - 1], "patch", (p + j) % patches,
        )

    to_mate = remote(own, mate_out, mate_sems.at[0], mate_sems.at[1], "patch", mate)
    kept = pl.ds(p * capacity, capacity)
    keep = pltpu.make_async_copy(coef.at[kept], arrived.at[kept], local_sem)

    @pl.when(crosses)
    def _():
        for k in range(per):
            crossing(k).start()

    to_mate.start()
    keep.start()

    @pl.when(crosses)
    def _():
        for k in range(per):
            crossing(k).wait_recv()

            @pl.when(not_last)
            def _():
                pass_on(True, c, k).start()

            @pl.when(not_first)
            def _():
                pass_on(False, c, k).start()


    to_mate.wait_recv()
    for j in range(1, patches):
        coefficients(j).start()

    @pl.when(crosses)
    def _():
        for j in range(1, cols):
            for k in range(per):
                below, above = c - j, c + j

                @pl.when(below >= 0)
                def _():
                    pass_on(True, below, k).wait_recv()

                    @pl.when(not_last)
                    def _():
                        pass_on(True, below, k).start()

                @pl.when(above < cols)
                def _():
                    pass_on(False, above, k).wait_recv()

                    @pl.when(not_first)
                    def _():
                        pass_on(False, above, k).start()

        for k in range(per):
            crossing(k).wait_send()
            for j in range(cols):
                below, above = c - j, c + j

                @pl.when(jnp.logical_and(below >= 0, not_last))
                def _():
                    pass_on(True, below, k).wait_send()

                @pl.when(jnp.logical_and(above < cols, not_first))
                def _():
                    pass_on(False, above, k).wait_send()

    keep.wait()
    to_mate.wait_send()
    for j in range(1, patches):
        coefficients_in(j).wait_recv()
        coefficients(j).wait_send()


def exchange_step(patches, cols, own, coef):
    per = own.shape[0] // cols
    dma = pltpu.SemaphoreType.DMA
    return pl.pallas_call(
        functools.partial(exchange_kernel, patches, cols),
        in_specs=[pl.BlockSpec(memory_space=pl.ANY)] * 2,
        out_specs=[pl.BlockSpec(memory_space=pl.ANY)] * 3,
        out_shape=[
            jax.ShapeDtypeStruct(own.shape, own.dtype),
            jax.ShapeDtypeStruct(own.shape, own.dtype),
            jax.ShapeDtypeStruct(coef.shape, coef.dtype),
        ],
        scratch_shapes=[
            dma((2,)),
            dma((per,)),
            dma((per,)),
            dma((cols, per)),
            dma((cols, per)),
            dma((cols, per)),
            dma((patches - 1,)),
            dma((patches - 1,)),
            dma(()),
        ],
        compiler_params=pltpu.CompilerParams(
            collective_id=0, has_side_effects=True, vmem_limit_bytes=8 * MIB
        ),
        name="exchange",
    )(own, coef)


def line_kernel(
    cols, part_ref, out_ref, up_in, up_out, down_in, down_out,
    up_send, up_recv, down_send, down_recv,
):
    me = lax.axis_index("col")
    width = part_ref.shape[3] // PIECES
    not_first = me > 0
    not_last = me < cols - 1

    barrier = pltpu.get_barrier_semaphore()

    @pl.when(not_first)
    def _():
        pl.semaphore_signal(barrier, inc=1, device_id={"col": me - 1}, device_id_type=MESH)

    @pl.when(not_last)
    def _():
        pl.semaphore_signal(barrier, inc=1, device_id={"col": me + 1}, device_id_type=MESH)

    pl.semaphore_wait(barrier, jnp.where(jnp.logical_and(not_first, not_last), 2, 1))

    def span(k):
        return pl.ds(pl.multiple_of(k * width, width), width)

    def hop(up, d, k):
        out, into = (up_out, up_in) if up else (down_out, down_in)
        send, recv = (up_send, up_recv) if up else (down_send, down_recv)
        peer = me + 1 if up else me - 1
        piece = (d, slice(None), slice(None), span(k))
        return remote(out.at[piece], into.at[piece], send.at[d, k], recv.at[d, k], "col", peer)

    def step(up, d, k):
        out, into = (up_out, up_in) if up else (down_out, down_in)
        more = not_first if up else not_last
        piece = (d, slice(None), slice(None), span(k))

        @pl.when(more)
        def _():
            hop(up, d, k).wait_recv()
            total = part_ref[piece].astype(jnp.float32) + into[piece].astype(jnp.float32)
            out[piece] = total.astype(jnp.bfloat16)

        @pl.when(jnp.logical_not(more))
        def _():
            out[piece] = part_ref[piece]

        hop(up, d, k).start()

    count = (cols - 1) * PIECES
    up_first = me < cols - 1 - me

    def send_all(i, carry):
        j, k = i // PIECES, i % PIECES
        high, low = cols - 1 - j, j
        sends_up = high > me
        sends_down = low < me

        @pl.when(jnp.logical_and(sends_up, up_first))
        def _():
            step(True, high, k)

        @pl.when(sends_down)
        def _():
            step(False, low, k)

        @pl.when(jnp.logical_and(sends_up, jnp.logical_not(up_first)))
        def _():
            step(True, high, k)

        return carry

    lax.fori_loop(0, count, send_all, 0)

    def finish(k, carry):
        piece = (me, slice(None), slice(None), span(k))
        goal = (slice(None), slice(None), span(k))
        out_ref[goal] = part_ref[piece].astype(jnp.float32)

        @pl.when(not_first)
        def _():
            hop(True, me, k).wait_recv()
            out_ref[goal] += up_in[piece].astype(jnp.float32)

        @pl.when(not_last)
        def _():
            hop(False, me, k).wait_recv()
            out_ref[goal] += down_in[piece].astype(jnp.float32)

        return carry

    lax.fori_loop(0, PIECES, finish, 0)

    def settle(i, carry):
        j, k = i // PIECES, i % PIECES
        high, low = cols - 1 - j, j

        @pl.when(high > me)
        def _():
            hop(True, high, k).wait_send()

        @pl.when(low < me)
        def _():
            hop(False, low, k).wait_send()

        return carry

    lax.fori_loop(0, count, settle, 0)


def line_step(partial):
    cols, _, sub, row_cells = partial.shape
    dma = pltpu.SemaphoreType.DMA
    return pl.pallas_call(
        functools.partial(line_kernel, cols),
        in_specs=[pl.BlockSpec(memory_space=pltpu.VMEM)],
        out_specs=pl.BlockSpec(memory_space=pltpu.VMEM),
        out_shape=jax.ShapeDtypeStruct((3, sub, row_cells), jnp.float32),
        scratch_shapes=[pltpu.VMEM(partial.shape, jnp.bfloat16)] * 4 + [dma((cols, PIECES))] * 4,
        compiler_params=pltpu.CompilerParams(
            collective_id=1, has_side_effects=True, vmem_limit_bytes=32 * MIB
        ),
        name="line",
    )(partial)


def shards(
    velocity,
    state,
    friction,
    near_src,
    near_block,
    far_dest,
    far_rank,
    far_basis_v,
    far_target,
    far_basis_u,
):
    members, _, row_cells = velocity.shape
    clusters = row_cells // CS
    near_count = near_src.shape[1]
    far_count = far_dest.shape[2]
    rank_width, width = far_basis_v.shape[3:]
    patches = lax.axis_size("patch")
    shares = lax.axis_size("col")
    capacity = far_target.shape[3]
    slots = patches * capacity
    member_share = state.shape[0]
    sub = member_share // CHUNKS
    planes = jnp.transpose(velocity, (1, 0, 2))
    split = planes.reshape(3, shares, CHUNKS, sub, row_cells)
    basis_v = far_basis_v.reshape(clusters, far_count * rank_width, width)
    basis_u = far_basis_u.reshape(slots, rank_width, width)
    blocks = near_block
    dest = far_dest.reshape(-1)
    rank = far_rank.reshape(-1)
    target = far_target.reshape(-1)
    at_patch = lax.axis_index("patch")
    offset = near_src - (at_patch - 1) * clusters
    row, cell = offset // clusters, offset % clusters
    row = jnp.where(at_patch % 2 == 0, 2 - row, row)
    src = (row * clusters + cell).reshape(-1)
    own, coef = source_step(0, split, basis_v, dest, rank)(slots)
    mate, cross, arrived = exchange_step(patches, shares, own, coef)
    partial = target_step(shares, src, target, mate, own, cross, blocks, arrived, basis_u)
    parts = [line_step(partial)[None]]
    col = lax.axis_index("col").reshape(1).astype(jnp.int32)
    rate = law_step(col, parts, planes, state, friction)
    return jnp.transpose(rate, (1, 0, 2))


def solution(mesh):
    return jax.shard_map(
        shards,
        mesh=mesh,
        in_specs=(
            P("runs", None, "patch"),
            P(("runs", "col"), "patch"),
            P("runs", "patch"),
            P("patch", "col"),
            P("patch", "col", None, None),
            P("col", "patch", None),
            P("col", "patch", None),
            P("col", "patch", None, None, None),
            P("col", "patch", None, None),
            P("col", "patch", None, None, None, None),
        ),
        out_specs=P(("runs", "col"), None, "patch"),
        check_vma=False,
    )
```

```python
import functools
import jax
import jax.numpy as jnp
from jax import lax
from jax.experimental import pallas as pl
from jax.experimental.pallas import tpu as pltpu
from jax.sharding import PartitionSpec as P

CS = 128
CHUNKS = 1
PIECES = 4
GROUP = 8
MIB = 1 << 20
MESH = pl.DeviceIdType.MESH

damping = 0.5
speed_floor = 0.25

NT = (((1,), (1,)), ((), ()))
TN = (((0,), (0,)), ((), ()))


def source_kernel(far_count, rank_width, dest_ref, rank_ref, vel_ref, basis_ref, own_ref, coef_ref):
    g = pl.program_id(0)
    members = own_ref.shape[1]
    for c in range(3):
        part = vel_ref[c].reshape(members, CS).astype(jnp.bfloat16)
        own_ref[0, :, c * CS : (c + 1) * CS] = part
    raw = lax.dot_general(basis_ref[0], own_ref[0], NT, preferred_element_type=jnp.float32)
    rows = lax.broadcasted_iota(jnp.int32, (rank_width, members), 0)
    for j in range(far_count):
        block = raw[j * rank_width : (j + 1) * rank_width]
        block = jnp.where(rows < rank_ref[g * far_count + j], block, 0.0)
        coef_ref[dest_ref[g * far_count + j]] = block.astype(jnp.bfloat16)


def source_step(chunk, velocity, basis_v, dest, rank):
    _, shares, _, sub, row_cells = velocity.shape
    members = shares * sub
    clusters = row_cells // CS
    far_count = dest.shape[0] // clusters
    rank_width = basis_v.shape[1] // far_count
    width = basis_v.shape[2]

    def call(slots):
        return pl.pallas_call(
            functools.partial(source_kernel, far_count, rank_width),
            grid_spec=pltpu.PrefetchScalarGridSpec(
                num_scalar_prefetch=2,
                grid=(clusters,),
                in_specs=[
                    pl.BlockSpec((3, shares, None, sub, CS), lambda g, *_: (0, 0, chunk, 0, g)),
                    pl.BlockSpec((1, far_count * rank_width, width), lambda g, *_: (g, 0, 0)),
                ],
                out_specs=[
                    pl.BlockSpec((1, members, width), lambda g, *_: (g, 0, 0)),
                    pl.BlockSpec((slots, rank_width, members), lambda g, *_: (0, 0, 0)),
                ],
            ),
            out_shape=[
                jax.ShapeDtypeStruct((clusters, members, width), jnp.bfloat16),
                jax.ShapeDtypeStruct((slots, rank_width, members), jnp.bfloat16),
            ],
            compiler_params=pltpu.CompilerParams(vmem_limit_bytes=24 * MIB),
            cost_estimate=pl.CostEstimate(
                flops=2 * clusters * far_count * rank_width * width * members,
                bytes_accessed=8 * MIB,
                transcendentals=0,
            ),
            name="source",
        )(dest, rank, velocity, basis_v)

    return call


def target_kernel(
    near_count, rank_width, src_ref, target_ref,
    mate_ref, own_ref, cross_ref, block_ref, coef_ref, basis_ref,
    out_ref, cells, acc, picked_c, picked_u, slot_list, slot_count, sems,
):
    t = pl.program_id(0)
    clusters = own_ref.shape[0]
    slots = coef_ref.shape[0]
    shares, _, sub, _ = out_ref.shape

    @pl.when(t == 0)
    def _():
        copies = [
            pltpu.make_async_copy(ref, cells.at[pl.ds(i * clusters, clusters)], sems.at[i])
            for i, ref in enumerate((mate_ref, own_ref, cross_ref))
        ]
        for copy in copies:
            copy.start()

        def clear(i, carry):
            slot_count[i] = 0
            return carry

        lax.fori_loop(0, clusters, clear, 0)

        def place(s, carry):
            goal = target_ref[s]

            @pl.when(goal >= 0)
            def _():
                at = slot_count[goal]
                slot_list[goal * slots + at] = s
                slot_count[goal] = at + 1

            return carry

        lax.fori_loop(0, slots, place, 0)
        for copy in copies:
            copy.wait()

    total = None
    for j in range(near_count):
        cell = cells[src_ref[t * near_count + j]]
        part = lax.dot_general(cell, block_ref[0, j], NT, preferred_element_type=jnp.float32)
        total = part if total is None else total + part
    acc[...] = total
    count = slot_count[t]

    def group(i, carry):
        for j in range(GROUP):
            at = i * GROUP + j
            live = at < count
            s = slot_list[t * slots + jnp.where(live, at, 0)]
            s = jnp.where(live, s, 0)
            piece = pl.ds(j * rank_width, rank_width)
            coef = coef_ref[s]
            picked_c[piece, :] = jnp.where(live, coef, jnp.zeros_like(coef))
            picked_u[piece, :] = basis_ref[s]
        acc[...] += lax.dot_general(
            picked_c[...], picked_u[...], TN, preferred_element_type=jnp.float32
        )
        return carry

    lax.fori_loop(0, (count + GROUP - 1) // GROUP, group, 0)
    for d in range(shares):
        for c in range(3):
            out_ref[d, c] = acc[d * sub : (d + 1) * sub, c * CS : (c + 1) * CS].astype(jnp.bfloat16)


def target_step(shares, src, target, mate, own, cross, blocks, coef, basis_u):
    clusters, members, width = own.shape
    near_count = blocks.shape[1]
    slots, rank_width, _ = coef.shape
    sub = members // shares
    whole = lambda t, *_: (0, 0, 0)
    return pl.pallas_call(
        functools.partial(target_kernel, near_count, rank_width),
        grid_spec=pltpu.PrefetchScalarGridSpec(
            num_scalar_prefetch=2,
            grid=(clusters,),
            in_specs=[
                pl.BlockSpec(memory_space=pl.ANY),
                pl.BlockSpec(memory_space=pl.ANY),
                pl.BlockSpec(memory_space=pl.ANY),
                pl.BlockSpec((1, near_count, width, width), lambda t, *_: (t, 0, 0, 0)),
                pl.BlockSpec((slots, rank_width, members), whole),
                pl.BlockSpec((slots, rank_width, width), whole),
            ],
            out_specs=pl.BlockSpec((shares, 3, sub, CS), lambda t, *_: (0, 0, 0, t)),
            scratch_shapes=[
                pltpu.VMEM((3 * clusters, members, width), jnp.bfloat16),
                pltpu.VMEM((members, width), jnp.float32),
                pltpu.VMEM((GROUP * rank_width, members), jnp.bfloat16),
                pltpu.VMEM((GROUP * rank_width, width), jnp.bfloat16),
                pltpu.SMEM((clusters * slots,), jnp.int32),
                pltpu.SMEM((clusters,), jnp.int32),
                pltpu.SemaphoreType.DMA((3,)),
            ],
        ),
        out_shape=jax.ShapeDtypeStruct((shares, 3, sub, clusters * CS), jnp.bfloat16),
        compiler_params=pltpu.CompilerParams(vmem_limit_bytes=36 * MIB),
        cost_estimate=pl.CostEstimate(
            flops=2 * clusters * members * width * (near_count * width + GROUP * rank_width),
            bytes_accessed=24 * MIB,
            transcendentals=0,
        ),
        name="target",
    )(src, target, mate, own, cross, blocks, coef, basis_u)


def law_kernel(chunks, col_ref, *refs):
    parts = refs[:chunks]
    vel_ref, state_ref, friction_ref, out_ref = refs[chunks:]
    sub = parts[0].shape[2]
    for h in range(chunks):
        rows = slice(h * sub, (h + 1) * sub)
        velocity = [vel_ref[c, rows, :] for c in range(3)]
        speed = jnp.sqrt(
            velocity[0] * velocity[0] + velocity[1] * velocity[1] + velocity[2] * velocity[2] + speed_floor
        )
        state = state_ref[rows, :]
        state_rate = 1.0 - speed * state / friction_ref[2:3, :]
        pulled = friction_ref[1:2, :] * state_rate / (state * speed)
        below = friction_ref[0:1, :] / speed + damping
        for c in range(3):
            stress = jnp.sum(parts[h][:, c].astype(jnp.float32), axis=0)
            out_ref[c, rows, :] = (-stress - pulled * velocity[c]) / below


def law_step(col, parts, velocity, state, friction):
    member_share, row_cells = state.shape
    chunks = len(parts)
    shares, _, sub, _ = parts[0].shape
    tile = min(512, row_cells)
    return pl.pallas_call(
        functools.partial(law_kernel, chunks),
        grid_spec=pltpu.PrefetchScalarGridSpec(
            num_scalar_prefetch=1,
            grid=(row_cells // tile,),
            in_specs=[pl.BlockSpec((shares, 3, sub, tile), lambda e, col: (0, 0, 0, e))] * chunks
            + [
                pl.BlockSpec((3, member_share, tile), lambda e, col: (0, col[0], e)),
                pl.BlockSpec((member_share, tile), lambda e, col: (0, e)),
                pl.BlockSpec((3, tile), lambda e, col: (0, e)),
            ],
            out_specs=pl.BlockSpec((3, member_share, tile), lambda e, col: (0, 0, e)),
        ),
        out_shape=jax.ShapeDtypeStruct((3, member_share, row_cells), jnp.float32),
        compiler_params=pltpu.CompilerParams(vmem_limit_bytes=24 * MIB),
        cost_estimate=pl.CostEstimate(flops=MIB * 16, bytes_accessed=8 * MIB, transcendentals=0),
        name="law",
    )(col, *parts, velocity, state, friction)


def remote(src, dst, send, recv, axis, peer):
    return pltpu.make_async_remote_copy(
        src_ref=src,
        dst_ref=dst,
        send_sem=send,
        recv_sem=recv,
        device_id={axis: peer},
        device_id_type=MESH,
    )


def exchange_kernel(
    patches, cols, own, coef, mate_out, cross_out, arrived,
    mate_sems, cross_send, cross_recv, up_send, down_send, share_recv, coef_send, coef_recv, local_sem,
):
    p = lax.axis_index("patch")
    c = lax.axis_index("col")
    odd = p % 2
    mate = p + 1 - 2 * odd
    cross = p + 2 * odd - 1
    crosses = jnp.logical_and(cross >= 0, cross < patches)
    per = own.shape[0] // cols
    capacity = coef.shape[0] // patches

    barrier = pltpu.get_barrier_semaphore()
    for j in range(1, patches):
        pl.semaphore_signal(barrier, inc=1, device_id={"patch": (p + j) % patches}, device_id_type=MESH)
    for j in range(1, cols):
        pl.semaphore_signal(barrier, inc=1, device_id={"col": (c + j) % cols}, device_id_type=MESH)
    pl.semaphore_wait(barrier, patches + cols - 2)

    def crossing(k):
        at = c * per + k
        return remote(own.at[at], cross_out.at[at], cross_send.at[k], cross_recv.at[k], "patch", cross)

    def pass_on(up, source, k):
        at = source * per + k
        send = up_send if up else down_send
        peer = c + 1 if up else c - 1
        return remote(
            cross_out.at[at], cross_out.at[at], send.at[source, k], share_recv.at[source, k], "col", peer
        )

    not_first = c > 0
    not_last = c < cols - 1

    def coefficients(j):
        q = (p + j) % patches
        return remote(
            coef.at[pl.ds(q * capacity, capacity)], arrived.at[pl.ds(p * capacity, capacity)],
            coef_send.at[j - 1], coef_recv.at[j - 1], "patch", q,
        )

    def coefficients_in(j):
        q = (p + patches - j) % patches
        return remote(
            coef.at[pl.ds(q * capacity, capacity)], arrived.at[pl.ds(q * capacity, capacity)],
            coef_send.at[j - 1], coef_recv.at[j - 1], "patch", (p + j) % patches,
        )

    to_mate = remote(own, mate_out, mate_sems.at[0], mate_sems.at[1], "patch", mate)
    kept = pl.ds(p * capacity, capacity)
    keep = pltpu.make_async_copy(coef.at[kept], arrived.at[kept], local_sem)

    @pl.when(crosses)
    def _():
        for k in range(per):
            crossing(k).start()

    to_mate.start()
    keep.start()

    @pl.when(crosses)
    def _():
        for k in range(per):
            crossing(k).wait_recv()

            @pl.when(not_last)
            def _():
                pass_on(True, c, k).start()

            @pl.when(not_first)
            def _():
                pass_on(False, c, k).start()


    to_mate.wait_recv()
    for j in range(1, patches):
        coefficients(j).start()

    @pl.when(crosses)
    def _():
        for j in range(1, cols):
            for k in range(per):
                below, above = c - j, c + j

                @pl.when(below >= 0)
                def _():
                    pass_on(True, below, k).wait_recv()

                    @pl.when(not_last)
                    def _():
                        pass_on(True, below, k).start()

                @pl.when(above < cols)
                def _():
                    pass_on(False, above, k).wait_recv()

                    @pl.when(not_first)
                    def _():
                        pass_on(False, above, k).start()

        for k in range(per):
            crossing(k).wait_send()
            for j in range(cols):
                below, above = c - j, c + j

                @pl.when(jnp.logical_and(below >= 0, not_last))
                def _():
                    pass_on(True, below, k).wait_send()

                @pl.when(jnp.logical_and(above < cols, not_first))
                def _():
                    pass_on(False, above, k).wait_send()

    keep.wait()
    to_mate.wait_send()
    for j in range(1, patches):
        coefficients_in(j).wait_recv()
        coefficients(j).wait_send()


def exchange_step(patches, cols, own, coef):
    per = own.shape[0] // cols
    dma = pltpu.SemaphoreType.DMA
    return pl.pallas_call(
        functools.partial(exchange_kernel, patches, cols),
        in_specs=[pl.BlockSpec(memory_space=pl.ANY)] * 2,
        out_specs=[pl.BlockSpec(memory_space=pl.ANY)] * 3,
        out_shape=[
            jax.ShapeDtypeStruct(own.shape, own.dtype),
            jax.ShapeDtypeStruct(own.shape, own.dtype),
            jax.ShapeDtypeStruct(coef.shape, coef.dtype),
        ],
        scratch_shapes=[
            dma((2,)),
            dma((per,)),
            dma((per,)),
            dma((cols, per)),
            dma((cols, per)),
            dma((cols, per)),
            dma((patches - 1,)),
            dma((patches - 1,)),
            dma(()),
        ],
        compiler_params=pltpu.CompilerParams(
            collective_id=0, has_side_effects=True, vmem_limit_bytes=8 * MIB
        ),
        name="exchange",
    )(own, coef)


def line_kernel(
    cols, part_ref, out_ref, up_in, up_out, down_in, down_out,
    up_send, up_recv, down_send, down_recv,
):
    me = lax.axis_index("col")
    width = part_ref.shape[3] // PIECES
    not_first = me > 0
    not_last = me < cols - 1

    barrier = pltpu.get_barrier_semaphore()

    @pl.when(not_first)
    def _():
        pl.semaphore_signal(barrier, inc=1, device_id={"col": me - 1}, device_id_type=MESH)

    @pl.when(not_last)
    def _():
        pl.semaphore_signal(barrier, inc=1, device_id={"col": me + 1}, device_id_type=MESH)

    pl.semaphore_wait(barrier, jnp.where(jnp.logical_and(not_first, not_last), 2, 1))

    def span(k):
        return pl.ds(pl.multiple_of(k * width, width), width)

    def hop(up, d, k):
        out, into = (up_out, up_in) if up else (down_out, down_in)
        send, recv = (up_send, up_recv) if up else (down_send, down_recv)
        peer = me + 1 if up else me - 1
        piece = (d, slice(None), slice(None), span(k))
        return remote(out.at[piece], into.at[piece], send.at[d, k], recv.at[d, k], "col", peer)

    def step(up, d, k):
        out, into = (up_out, up_in) if up else (down_out, down_in)
        more = not_first if up else not_last
        piece = (d, slice(None), slice(None), span(k))

        @pl.when(more)
        def _():
            hop(up, d, k).wait_recv()
            total = part_ref[piece].astype(jnp.float32) + into[piece].astype(jnp.float32)
            out[piece] = total.astype(jnp.bfloat16)

        @pl.when(jnp.logical_not(more))
        def _():
            out[piece] = part_ref[piece]

        hop(up, d, k).start()

    count = (cols - 1) * PIECES
    up_first = me < cols - 1 - me

    def send_all(i, carry):
        j, k = i // PIECES, i % PIECES
        high, low = cols - 1 - j, j
        sends_up = high > me
        sends_down = low < me

        @pl.when(jnp.logical_and(sends_up, up_first))
        def _():
            step(True, high, k)

        @pl.when(sends_down)
        def _():
            step(False, low, k)

        @pl.when(jnp.logical_and(sends_up, jnp.logical_not(up_first)))
        def _():
            step(True, high, k)

        return carry

    lax.fori_loop(0, count, send_all, 0)

    def finish(k, carry):
        piece = (me, slice(None), slice(None), span(k))
        goal = (slice(None), slice(None), span(k))
        out_ref[goal] = part_ref[piece].astype(jnp.float32)

        @pl.when(not_first)
        def _():
            hop(True, me, k).wait_recv()
            out_ref[goal] += up_in[piece].astype(jnp.float32)

        @pl.when(not_last)
        def _():
            hop(False, me, k).wait_recv()
            out_ref[goal] += down_in[piece].astype(jnp.float32)

        return carry

    lax.fori_loop(0, PIECES, finish, 0)

    def settle(i, carry):
        j, k = i // PIECES, i % PIECES
        high, low = cols - 1 - j, j

        @pl.when(high > me)
        def _():
            hop(True, high, k).wait_send()

        @pl.when(low < me)
        def _():
            hop(False, low, k).wait_send()

        return carry

    lax.fori_loop(0, count, settle, 0)


def line_step(partial):
    cols, _, sub, row_cells = partial.shape
    dma = pltpu.SemaphoreType.DMA
    return pl.pallas_call(
        functools.partial(line_kernel, cols),
        in_specs=[pl.BlockSpec(memory_space=pltpu.VMEM)],
        out_specs=pl.BlockSpec(memory_space=pltpu.VMEM),
        out_shape=jax.ShapeDtypeStruct((3, sub, row_cells), jnp.float32),
        scratch_shapes=[pltpu.VMEM(partial.shape, jnp.bfloat16)] * 4 + [dma((cols, PIECES))] * 4,
        compiler_params=pltpu.CompilerParams(
            collective_id=1, has_side_effects=True, vmem_limit_bytes=32 * MIB
        ),
        name="line",
    )(partial)


def shards(
    velocity,
    state,
    friction,
    near_src,
    near_block,
    far_dest,
    far_rank,
    far_basis_v,
    far_target,
    far_basis_u,
):
    members, _, row_cells = velocity.shape
    clusters = row_cells // CS
    near_count = near_src.shape[1]
    far_count = far_dest.shape[2]
    rank_width, width = far_basis_v.shape[3:]
    patches = lax.axis_size("patch")
    shares = lax.axis_size("col")
    capacity = far_target.shape[3]
    slots = patches * capacity
    member_share = state.shape[0]
    sub = member_share // CHUNKS
    planes = jnp.transpose(velocity, (1, 0, 2))
    split = planes.reshape(3, shares, CHUNKS, sub, row_cells)
    basis_v = far_basis_v.reshape(clusters, far_count * rank_width, width)
    basis_u = far_basis_u.reshape(slots, rank_width, width)
    blocks = near_block
    dest = far_dest.reshape(-1)
    rank = far_rank.reshape(-1)
    target = far_target.reshape(-1)
    at_patch = lax.axis_index("patch")
    offset = near_src - (at_patch - 1) * clusters
    row, cell = offset // clusters, offset % clusters
    row = jnp.where(at_patch % 2 == 0, 2 - row, row)
    src = (row * clusters + cell).reshape(-1)
    own, coef = source_step(0, split, basis_v, dest, rank)(slots)
    mate, cross, arrived = exchange_step(patches, shares, own, coef)
    partial = target_step(shares, src, target, mate, own, cross, blocks, arrived, basis_u)
    parts = [line_step(partial)[None]]
    col = lax.axis_index("col").reshape(1).astype(jnp.int32)
    rate = law_step(col, parts, planes, state, friction)
    return jnp.transpose(rate, (1, 0, 2))


def solution(mesh):
    return jax.shard_map(
        shards,
        mesh=mesh,
        in_specs=(
            P("runs", None, "patch"),
            P(("runs", "col"), "patch"),
            P("runs", "patch"),
            P("patch", "col"),
            P("patch", "col", None, None),
            P("col", "patch", None),
            P("col", "patch", None),
            P("col", "patch", None, None, None),
            P("col", "patch", None, None),
            P("col", "patch", None, None, None, None),
        ),
        out_specs=P(("runs", "col"), None, "patch"),
        check_vma=False,
    )
```
